32 devices in a mesh: grp: 2 (over y), row: 8 (over z, x), col: 2 (over core).
Axes of the slice: x: 2, y: 2, z: 4, core: 2. Of those that a mesh axis runs over, the one named last changes fastest.
Arguments:
- blocks: bfloat16 [64, 256, 256], P(('grp', 'row', 'col')), parts along dimension 0, may hold values from -0.375 to 0.375
- virtual: bfloat16 [64, 256], P(('grp', 'row', 'col')), parts along dimension 0, may hold values from 0.5 to 3
- occupied: bfloat16 [64], P(('grp', 'row', 'col')), parts along dimension 0, may hold values from -1.5 to -0.29882812
- domains: int32 [64, 256], P('grp'), parts along dimension 0, may hold values from 0 to 383, as said below
- pair_list: int32 [512, 2], P(('grp', 'row', 'col')), parts along dimension 0, may hold values from -1 to 31, as said below
- coupling: float32 [512], P(('grp', 'row', 'col')), parts along dimension 0, may hold values from -3 to 3
Outputs:
- amplitudes: bfloat16 [512, 256, 256], P(('grp', 'row', 'col')), parts along dimension 0
- energies: float32 [512], P(('grp', 'row', 'col')), parts along dimension 0
The draws below stay inside these ranges and needn't reach their ends.
There are 2 independent parts, one for each index of `grp`. The reference program is written for one: setup_inputs(seed, part) draws one part's arguments, and reference() takes and returns one part's arrays. A program takes and returns all parts, laid end to end along the dimension named above; each array names one. Nothing has to cross between parts.
Inputs may be any that keep to these rules, and one draw needn't show every extreme that they name: `pair_list`: live pairs come first in each device's 16 slots and empty slots hold -1 twice. A pair on the device at some row and col has its first orbital among the orbitals owned by the devices of that row and its second among the orbitals owned by devices of that col; on one device no more than 2 live pairs have second orbitals owned on one row, and some device has all its slots live. No pair appears twice on a device. `domains`: each row holds 256 distinct indices in increasing order.
All inputs are finite; a program needn't handle non-finite values.
Results may differ from the reference program's by a relative error of at most 0.0045.
Values may be sent and summed in bfloat16 or wider, within the bound.
A program may use at most 128 MiB of HBM per device.

```python
import math
import jax
import jax.numpy as jnp
from jax import lax

P_SIZE = 256
NAUXL = 256
OCC_DEV = 2
PAIR_DEV = 16
NOCC = 32
NPAIR = 256
NPAO = 384
JCAP = 2
N_ROW = 8
N_COL = 2


def draw_pairs_core(key):
    device_total = N_ROW * N_COL
    groups = (PAIR_DEV + JCAP - 1) // JCAP
    combos = N_COL * OCC_DEV * OCC_DEV
    full_key, level_key, device_key = jax.random.split(key, 3)
    full_device = jax.random.randint(full_key, (), 0, device_total)
    levels = jax.random.randint(level_key, (device_total,), 2, 4)
    counts = PAIR_DEV // 8 * 2 ** levels
    counts = jnp.where(jnp.arange(device_total) == full_device, PAIR_DEV, counts)

    def one_device(dev_key, device, count):
        row_key, combo_key = jax.random.split(dev_key)
        owner_rows = jax.random.permutation(row_key, N_ROW)[:groups]
        combo_keys = jax.random.split(combo_key, groups)
        picks = jax.vmap(lambda sub: jax.random.permutation(sub, combos)[:JCAP])(combo_keys)
        slot_ids = jnp.arange(PAIR_DEV)
        group_ids = slot_ids // JCAP
        within = slot_ids % JCAP
        owner = owner_rows[group_ids]
        combo = picks[group_ids, within]
        row_here = device // N_COL
        col_here = device % N_COL
        first_orb = row_here * N_COL * OCC_DEV + combo // OCC_DEV
        second_orb = (owner * N_COL + col_here) * OCC_DEV + combo % OCC_DEV
        used = slot_ids < count
        return jnp.stack([jnp.where(used, first_orb, -1), jnp.where(used, second_orb, -1)], axis=1)
    result = jax.vmap(one_device)(jax.random.split(device_key, device_total), jnp.arange(device_total), counts)
    return result.reshape(device_total * PAIR_DEV, 2).astype(jnp.int32)


def draw_pair_list(key, part):
    key = jax.random.fold_in(key, 11)
    return draw_pairs_core(key)


def draw_domains(key, part):
    key = jax.random.fold_in(key, 13)
    keys = jax.random.split(key, NOCC)
    picked = jax.vmap(lambda sub: jnp.sort(jax.random.permutation(sub, NPAO)[:P_SIZE]))(keys)
    return picked.astype(jnp.int32)


def block_levels(rng, extent, cuts, low, top_value):
    loudness = 1.0
    for dim, shards_of in cuts:
        steps = jax.random.uniform(jax.random.fold_in(jax.random.fold_in(rng, 6), dim), (shards_of,), jnp.float32, low / len(cuts), top_value / len(cuts))
        loudness = loudness * jnp.repeat(jnp.exp(steps), extent[dim] // shards_of).reshape((-1,) + (1,) * (len(extent) - 1 - dim))
    return loudness


def centred(rng, extent, width, most, cuts=(), held_as=jnp.bfloat16):
    values = width * jax.random.normal(rng, extent, jnp.float32)
    if cuts:
        values = values * block_levels(rng, extent, cuts, -0.22, 0.18)
    return jnp.clip(values, -most, most).astype(held_as)


def setup_inputs(seed: int = 0, part: int = 0) -> dict:
    key_list = jax.random.split(jax.random.key(seed), 7)
    part_keys = jax.random.split(jax.random.fold_in(key_list[6], part), 7)
    return {
        "blocks": centred(part_keys[0], (NOCC, NAUXL, P_SIZE), NAUXL ** -0.5, 0.375, ((0, 16),)),
        "virtual": jnp.clip(jnp.exp(math.log(3.0) - 1.7917595 * jax.random.uniform(part_keys[1], (NOCC, P_SIZE), jnp.float32) ** block_levels(part_keys[1], (NOCC, P_SIZE), ((0, 16),), -0.2, 0.2)), 0.5, 3.0).astype(jnp.bfloat16),
        "occupied": jnp.clip(-1.5 + 1.2011719 * jax.random.uniform(part_keys[2], (NOCC,), jnp.float32) ** block_levels(part_keys[2], (NOCC,), ((0, 16),), -0.2, 0.2), -1.5, -0.29882812).astype(jnp.bfloat16),
        "domains": draw_domains(jax.random.fold_in(jax.random.fold_in(key_list[6], part), 71), part),
        "pair_list": draw_pair_list(jax.random.fold_in(jax.random.fold_in(key_list[6], part), 71), part),
        "coupling": centred(part_keys[5], (NPAIR,), 0.5, 3.0, ((0, 16),), jnp.float32),
    }


def pair_maps(dom_left, dom_right):
    position = jnp.searchsorted(dom_right, dom_left).astype(jnp.int32)
    position = jnp.clip(position, 0, dom_right.shape[0] - 1).astype(jnp.int32)
    valid = jnp.take(dom_right, position) == dom_left
    return position, valid


def reference(blocks, virtual, occupied, domains, pair_list, coupling):
    pair_total = pair_list.shape[0]
    orbital_total = blocks.shape[0]
    batches = pair_total // PAIR_DEV
    active = pair_list[:, 0] >= 0
    first_orb = jnp.maximum(pair_list[:, 0], 0).astype(jnp.int32)
    second_orb = jnp.maximum(pair_list[:, 1], 0).astype(jnp.int32)

    def shaped(values):
        return values.reshape((batches, PAIR_DEV) + values.shape[1:])

    def denominators(left_idx, right_idx):
        virt_left = virtual[left_idx].astype(jnp.float32)
        virt_right = virtual[right_idx].astype(jnp.float32)
        occ_left = occupied[left_idx].astype(jnp.float32)
        occ_right = occupied[right_idx].astype(jnp.float32)
        return ((virt_left[:, :, None] + virt_right[:, None, :]) - occ_left[:, None, None]) - occ_right[:, None, None]

    def mapping(left_idx, right_idx):
        return jax.vmap(pair_maps)(domains[left_idx], domains[right_idx])

    def first_pass(carry, batch):
        row_table, col_table = carry
        left_idx, right_idx, mask, weight = batch
        integrals = jnp.einsum("pqa,pqb->pab", blocks[left_idx].astype(jnp.float32), blocks[right_idx].astype(jnp.float32))
        first_amp = -integrals / denominators(left_idx, right_idx)
        rounded = lax.optimization_barrier(first_amp.astype(jnp.bfloat16)).astype(jnp.float32)
        pos_ij, valid_ij = mapping(left_idx, right_idx)
        pos_ji, valid_ji = mapping(right_idx, left_idx)
        row_term = jnp.take_along_axis(rounded, jnp.broadcast_to(pos_ij[:, None, :], rounded.shape), axis=2)
        row_term = weight[:, None, None] * (row_term * valid_ij[:, None, :].astype(jnp.float32))
        col_term = jnp.take_along_axis(rounded, jnp.broadcast_to(pos_ji[:, :, None], rounded.shape), axis=1)
        col_term = weight[:, None, None] * (col_term * valid_ji[:, :, None].astype(jnp.float32))
        col_term = lax.optimization_barrier(col_term.astype(jnp.bfloat16)).astype(jnp.float32)
        keep = mask.astype(jnp.float32)[:, None, None]
        row_table = row_table.at[left_idx].add(row_term * keep)
        col_table = col_table.at[right_idx].add(col_term * keep)
        return (row_table, col_table), integrals

    empty = jnp.zeros((orbital_total, P_SIZE, P_SIZE), jnp.float32)
    (row_table, col_table), integrals = lax.scan(
        first_pass, (empty, empty),
        (shaped(first_orb), shaped(second_orb), shaped(active), shaped(coupling)))
    row_mix = lax.optimization_barrier(row_table.astype(jnp.bfloat16)).astype(jnp.float32)
    col_mix = lax.optimization_barrier(col_table.astype(jnp.bfloat16)).astype(jnp.float32)

    def second_pass(carry, batch):
        left_idx, right_idx, mask, integrals_now = batch
        pos_ij, valid_ij = mapping(left_idx, right_idx)
        pos_ji, valid_ji = mapping(right_idx, left_idx)
        col_part = col_mix[right_idx]
        row_part = row_mix[left_idx]
        from_col = jnp.take_along_axis(col_part, jnp.broadcast_to(pos_ij[:, :, None], col_part.shape), axis=1)
        from_col = from_col * valid_ij[:, :, None].astype(jnp.float32)
        from_row = jnp.take_along_axis(row_part, jnp.broadcast_to(pos_ji[:, None, :], row_part.shape), axis=2)
        from_row = from_row * valid_ji[:, None, :].astype(jnp.float32)
        second_amp = ((from_col + from_row) - integrals_now) / denominators(left_idx, right_idx)
        amps = jnp.where(mask[:, None, None], second_amp, 0.0).astype(jnp.bfloat16)
        energy = jnp.where(mask, jnp.sum(integrals_now * second_amp, axis=(1, 2)) / (P_SIZE * P_SIZE), 0.0).astype(jnp.float32)
        return carry, (amps, energy)

    _, (amplitudes, energies) = lax.scan(
        second_pass, jnp.zeros((), jnp.float32),
        (shaped(first_orb), shaped(second_orb), shaped(active), integrals))
    return amplitudes.reshape(pair_total, P_SIZE, P_SIZE), energies.reshape(pair_total)
```

```python
import functools
import jax
import jax.numpy as jnp
from jax import lax
from jax.experimental import pallas as pl
from jax.experimental.pallas import tpu as pltpu
from jax.sharding import PartitionSpec as P

FEAT = 16
UNROLL = 4
NT = (((1,), (1,)), ((), ()))
TN = (((0,), (0,)), ((), ()))
NN = (((1,), (0,)), ((), ()))


def mm(a, b, dims):
    return lax.dot_general(a, b, dims, preferred_element_type=jnp.float32)


def pair_kernel(
    dims,
    first_ref,
    second_ref,
    weight_ref,
    blocks_ref,
    left_ref,
    right_ref,
    amp_ref,
    energy_ref,
    col_acc,
    row_acc,
    slot_of,
    item_i,
    item_j,
    item_slot,
    item_w,
):
    row_count, col_count, occ_dev, pair_dev = dims
    my_row, my_col = lax.axis_index("row"), lax.axis_index("col")
    orbitals = row_count * col_count * occ_dev
    size = amp_ref.shape[1]
    mine = (my_row * col_count + my_col) * pair_dev
    near_base = my_row * col_count * occ_dev

    def clear(j, carry):
        slot_of[j] = -1
        return carry

    lax.fori_loop(0, orbitals, clear, 0)

    def claim(p, count):
        live = first_ref[mine + p] >= 0
        j = jnp.maximum(second_ref[mine + p], 0)
        fresh = live & (slot_of[j] < 0)

        @pl.when(fresh)
        def _():
            slot_of[j] = count

        return count + fresh.astype(jnp.int32)

    slots = lax.fori_loop(0, pair_dev, claim, jnp.int32(0))

    def count_live(base):
        def step(p, n):
            return n + (first_ref[base + p] >= 0).astype(jnp.int32)

        return lax.fori_loop(0, pair_dev, step, jnp.int32(0))

    def put(n, q, slot):
        item_i[n] = jnp.maximum(first_ref[q], 0)
        item_j[n] = jnp.maximum(second_ref[q], 0)
        item_slot[n] = slot
        item_w[n] = -weight_ref[q]

    def pad(n, slot):
        for u in range(UNROLL):
            item_i[n + u] = 0
            item_j[n + u] = 0
            item_slot[n + u] = slot
            item_w[n + u] = 0.0

    def zero_col(s, carry):
        col_acc[s] = jnp.zeros((size, size), jnp.float32)
        return carry

    lax.fori_loop(0, slots, zero_col, 0)
    row_acc[...] = jnp.zeros_like(row_acc)

    def first_amp(n):
        i, j, w = item_i[n], item_j[n], item_w[n]
        integ = mm(blocks_ref[i], blocks_ref[j], NT)
        denom = mm(left_ref[i], right_ref[j, :, :size], TN)
        gap = mm(left_ref[j], right_ref[i, :, size:], TN)
        match = jnp.where(gap == 0.0, 1.0, 0.0).astype(jnp.bfloat16)
        scaled = (integ * w) * pl.reciprocal(denom, approx=True)
        return scaled.astype(jnp.bfloat16), match

    def gather_items(q, n):
        owner = q // pair_dev
        at = (owner * col_count + my_col) * pair_dev + q % pair_dev
        j = jnp.maximum(second_ref[at], 0)
        slot = slot_of[j]
        take = (first_ref[at] >= 0) & (slot >= 0) & (owner != my_row)

        @pl.when(take)
        def _():
            put(n, at, slot)

        return n + take.astype(jnp.int32)

    total = lax.fori_loop(0, row_count * pair_dev, gather_items, jnp.int32(0))
    pad(total, 0)

    def col_step(t, carry):
        parts = [first_amp(t * UNROLL + u) for u in range(UNROLL)]
        terms = [mm(match, scaled, NN) for scaled, match in parts]
        for u in range(UNROLL):
            col_acc[item_slot[t * UNROLL + u]] += terms[u]
        return carry

    lax.fori_loop(0, (total + UNROLL - 1) // UNROLL, col_step, 0)

    def other_items(q, n):
        owner = q // pair_dev
        at = my_row * col_count * pair_dev + q
        take = (first_ref[at] >= 0) & (owner != my_col)

        @pl.when(take)
        def _():
            put(n, at, first_ref[at] - near_base)

        return n + take.astype(jnp.int32)

    total = lax.fori_loop(0, col_count * pair_dev, other_items, jnp.int32(0))
    pad(total, 0)

    def row_step(t, carry):
        parts = [first_amp(t * UNROLL + u) for u in range(UNROLL)]
        terms = [mm(scaled, match, NN) for scaled, match in parts]
        for u in range(UNROLL):
            row_acc[item_slot[t * UNROLL + u]] += terms[u]
        return carry

    lax.fori_loop(0, (total + UNROLL - 1) // UNROLL, row_step, 0)

    live_here = count_live(mine)

    def own_items(q, n):
        put(q, mine + q, slot_of[jnp.maximum(second_ref[mine + q], 0)])
        return n

    lax.fori_loop(0, live_here, own_items, 0)
    pad(live_here, 0)

    def own_step(t, carry):
        parts = [first_amp(t * UNROLL + u) for u in range(UNROLL)]
        col_terms = [mm(match, scaled, NN) for scaled, match in parts]
        row_terms = [mm(scaled, match, NN) for scaled, match in parts]
        for u in range(UNROLL):
            n = t * UNROLL + u
            col_acc[item_slot[n]] += col_terms[u]
            row_acc[jnp.clip(item_i[n] - near_base, 0, col_count * occ_dev - 1)] += row_terms[u]
        return carry

    lax.fori_loop(0, (live_here + UNROLL - 1) // UNROLL, own_step, 0)

    def second_step(p, carry):
        @pl.when(p < live_here)
        def _():
            i, j = item_i[p], item_j[p]
            integ = mm(blocks_ref[i], blocks_ref[j], NT)
            denom = mm(left_ref[i], right_ref[j, :, :size], TN)
            gap = mm(left_ref[i], right_ref[j, :, size:], TN)
            match = jnp.where(gap == 0.0, 1.0, 0.0).astype(jnp.bfloat16)
            col_mix = col_acc[item_slot[p]].astype(jnp.bfloat16)
            row_mix = row_acc[i - near_base].astype(jnp.bfloat16)
            mixed = mm(match, col_mix, NN) + mm(row_mix, match, NN)
            amp = (mixed - integ) * pl.reciprocal(denom, approx=True)
            amp_ref[p] = amp.astype(amp_ref.dtype)
            energy_ref[p] = jnp.sum(integ * amp) / (size * size)

        @pl.when(p >= live_here)
        def _():
            amp_ref[p] = jnp.zeros((size, size), amp_ref.dtype)
            energy_ref[p] = 0.0

        return carry

    lax.fori_loop(0, pair_dev, second_step, 0)


def features(virtual, occupied, domains):
    v = virtual.astype(jnp.float32)[:, None, :]
    o = occupied.astype(jnp.float32)[:, None, None]
    high = (domains // 256).astype(jnp.float32)[:, None, :]
    low = (domains % 256).astype(jnp.float32)[:, None, :]
    r = lax.broadcasted_iota(jnp.int32, (1, FEAT, 1), 1)

    def rows(entries):
        out = jnp.zeros((), jnp.float32)
        for k, e in enumerate(entries):
            if e is not None:
                out = jnp.where(r == k, e, out)
        shape = (v.shape[0], FEAT, v.shape[2])
        return jnp.broadcast_to(out, shape).astype(jnp.bfloat16)

    left = rows([v, 1.0, -o, 1.0, high, low, 1.0, 1.0])
    diff = rows([1.0, v, 1.0, -o])
    gap = rows([None] * 4 + [256.0, 1.0, -256.0 * high, -low])
    return left, jnp.concatenate([diff, gap], axis=2)


def shards(blocks, virtual, occupied, domains, pair_list, coupling):
    row_count, col_count = lax.axis_size("row"), lax.axis_size("col")
    occ_dev, fit, size = blocks.shape
    pair_dev = pair_list.shape[0]
    axes = ("row", "col")
    turned = jnp.swapaxes(blocks, 1, 2)
    all_blocks = lax.all_gather(turned, axes, axis=0, tiled=True)
    all_virtual = lax.all_gather(virtual, axes, axis=0, tiled=True)
    all_occupied = lax.all_gather(occupied, axes, axis=0, tiled=True)
    all_pairs = lax.all_gather(pair_list, axes, axis=0, tiled=True)
    all_weight = lax.all_gather(coupling, axes, axis=0, tiled=True)
    left, right = features(all_virtual, all_occupied, domains)
    smem = pl.BlockSpec(memory_space=pltpu.SMEM)
    vmem = pl.BlockSpec(memory_space=pltpu.VMEM)
    items = max(row_count, col_count) * pair_dev + UNROLL
    return pl.pallas_call(
        functools.partial(pair_kernel, (row_count, col_count, occ_dev, pair_dev)),
        out_shape=(
            jax.ShapeDtypeStruct((pair_dev, size, size), jnp.bfloat16),
            jax.ShapeDtypeStruct((pair_dev,), jnp.float32),
        ),
        in_specs=[smem] * 3 + [vmem] * 3,
        out_specs=(vmem, smem),
        scratch_shapes=[
            pltpu.VMEM((pair_dev, size, size), jnp.float32),
            pltpu.VMEM((col_count * occ_dev, size, size), jnp.float32),
            pltpu.SMEM((row_count * col_count * occ_dev,), jnp.int32),
            pltpu.SMEM((items,), jnp.int32),
            pltpu.SMEM((items,), jnp.int32),
            pltpu.SMEM((items,), jnp.int32),
            pltpu.SMEM((items,), jnp.float32),
        ],
        compiler_params=pltpu.CompilerParams(vmem_limit_bytes=56 * 1024 * 1024),
    )(all_pairs[:, 0], all_pairs[:, 1], all_weight, all_blocks, left, right)


def solution(mesh):
    return jax.shard_map(
        shards,
        mesh=mesh,
        in_specs=(
            P(("grp", "row", "col"), None, None),
            P(("grp", "row", "col"), None),
            P(("grp", "row", "col")),
            P("grp", None),
            P(("grp", "row", "col"), None),
            P(("grp", "row", "col")),
        ),
        out_specs=(P(("grp", "row", "col"), None, None), P(("grp", "row", "col"))),
        check_vma=False,
    )
```

```python
import functools
import jax
import jax.numpy as jnp
from jax import lax
from jax.experimental import pallas as pl
from jax.experimental.pallas import tpu as pltpu
from jax.sharding import PartitionSpec as P

FEAT = 16
UNROLL = 4
NT = (((1,), (1,)), ((), ()))
TN = (((0,), (0,)), ((), ()))
NN = (((1,), (0,)), ((), ()))


def mm(a, b, dims):
    return lax.dot_general(a, b, dims, preferred_element_type=jnp.float32)


def pair_kernel(
    dims,
    first_ref,
    second_ref,
    weight_ref,
    blocks_ref,
    amp_ref,
    energy_ref,
    col_acc,
    row_acc,
    slot_of,
    item_i,
    item_j,
    item_slot,
    item_w,
):
    row_count, col_count, occ_dev, pair_dev = dims
    my_row, my_col = lax.axis_index("row"), lax.axis_index("col")
    orbitals = row_count * col_count * occ_dev
    size = amp_ref.shape[1]
    mine = (my_row * col_count + my_col) * pair_dev
    near_base = my_row * col_count * occ_dev

    def clear(j, carry):
        slot_of[j] = -1
        return carry

    lax.fori_loop(0, orbitals, clear, 0)

    def claim(p, count):
        live = first_ref[mine + p] >= 0
        j = jnp.maximum(second_ref[mine + p], 0)
        fresh = live & (slot_of[j] < 0)

        @pl.when(fresh)
        def _():
            slot_of[j] = count

        return count + fresh.astype(jnp.int32)

    slots = lax.fori_loop(0, pair_dev, claim, jnp.int32(0))

    def count_live(base):
        def step(p, n):
            return n + (first_ref[base + p] >= 0).astype(jnp.int32)

        return lax.fori_loop(0, pair_dev, step, jnp.int32(0))

    def put(n, q, slot):
        item_i[n] = jnp.maximum(first_ref[q], 0)
        item_j[n] = jnp.maximum(second_ref[q], 0)
        item_slot[n] = slot
        item_w[n] = -weight_ref[q]

    def pad(n, slot):
        for u in range(UNROLL):
            item_i[n + u] = 0
            item_j[n + u] = 0
            item_slot[n + u] = slot
            item_w[n + u] = 0.0

    def zero_col(s, carry):
        col_acc[s] = jnp.zeros((size, size), jnp.float32)
        return carry

    lax.fori_loop(0, slots, zero_col, 0)
    row_acc[...] = jnp.zeros_like(row_acc)

    def block(o):
        return blocks_ref[o, :size, :]

    def features(o):
        f = blocks_ref[o, size:, :].astype(jnp.float32)
        left, right = f[:8], f[8:]
        top = lax.broadcasted_iota(jnp.int32, left.shape, 0) < 4
        halves = jnp.where(top, right, 0.0), jnp.where(top, 0.0, right)
        return left.astype(jnp.bfloat16), *(h.astype(jnp.bfloat16) for h in halves)

    def first_amp(n):
        i, j, w = item_i[n], item_j[n], item_w[n]
        integ = mm(block(i), block(j), NT)
        left_i, diff_i, gap_i = features(i)
        left_j, diff_j, gap_j = features(j)
        denom = mm(left_i, diff_j, TN)
        gap = mm(left_j, gap_i, TN)
        match = jnp.where(gap == 0.0, 1.0, 0.0).astype(jnp.bfloat16)
        scaled = (integ * w) * pl.reciprocal(denom, approx=True)
        return scaled.astype(jnp.bfloat16), match

    def gather_items(q, n):
        owner = q // pair_dev
        at = (owner * col_count + my_col) * pair_dev + q % pair_dev
        j = jnp.maximum(second_ref[at], 0)
        slot = slot_of[j]
        take = (first_ref[at] >= 0) & (slot >= 0) & (owner != my_row)

        @pl.when(take)
        def _():
            put(n, at, slot)

        return n + take.astype(jnp.int32)

    total = lax.fori_loop(0, row_count * pair_dev, gather_items, jnp.int32(0))
    pad(total, 0)

    def col_step(t, carry):
        parts = [first_amp(t * UNROLL + u) for u in range(UNROLL)]
        terms = [mm(match, scaled, NN) for scaled, match in parts]
        for u in range(UNROLL):
            col_acc[item_slot[t * UNROLL + u]] += terms[u]
        return carry

    lax.fori_loop(0, (total + UNROLL - 1) // UNROLL, col_step, 0)

    def other_items(q, n):
        owner = q // pair_dev
        at = my_row * col_count * pair_dev + q
        take = (first_ref[at] >= 0) & (owner != my_col)

        @pl.when(take)
        def _():
            put(n, at, first_ref[at] - near_base)

        return n + take.astype(jnp.int32)

    total = lax.fori_loop(0, col_count * pair_dev, other_items, jnp.int32(0))
    pad(total, 0)

    def row_step(t, carry):
        parts = [first_amp(t * UNROLL + u) for u in range(UNROLL)]
        terms = [mm(scaled, match, NN) for scaled, match in parts]
        for u in range(UNROLL):
            row_acc[item_slot[t * UNROLL + u]] += terms[u]
        return carry

    lax.fori_loop(0, (total + UNROLL - 1) // UNROLL, row_step, 0)

    live_here = count_live(mine)

    def own_items(q, n):
        put(q, mine + q, slot_of[jnp.maximum(second_ref[mine + q], 0)])
        return n

    lax.fori_loop(0, live_here, own_items, 0)
    pad(live_here, 0)

    def own_step(t, carry):
        parts = [first_amp(t * UNROLL + u) for u in range(UNROLL)]
        col_terms = [mm(match, scaled, NN) for scaled, match in parts]
        row_terms = [mm(scaled, match, NN) for scaled, match in parts]
        for u in range(UNROLL):
            n = t * UNROLL + u
            col_acc[item_slot[n]] += col_terms[u]
            row_acc[jnp.clip(item_i[n] - near_base, 0, col_count * occ_dev - 1)] += row_terms[u]
        return carry

    lax.fori_loop(0, (live_here + UNROLL - 1) // UNROLL, own_step, 0)

    def second_step(p, carry):
        @pl.when(p < live_here)
        def _():
            i, j = item_i[p], item_j[p]
            integ = mm(block(i), block(j), NT)
            left_i, diff_i, gap_i = features(i)
            left_j, diff_j, gap_j = features(j)
            denom = mm(left_i, diff_j, TN)
            gap = mm(left_i, gap_j, TN)
            match = jnp.where(gap == 0.0, 1.0, 0.0).astype(jnp.bfloat16)
            col_mix = col_acc[item_slot[p]].astype(jnp.bfloat16)
            row_mix = row_acc[i - near_base].astype(jnp.bfloat16)
            mixed = mm(match, col_mix, NN) + mm(row_mix, match, NN)
            amp = (mixed - integ) * pl.reciprocal(denom, approx=True)
            amp_ref[p] = amp.astype(amp_ref.dtype)
            energy_ref[p] = jnp.sum(integ * amp) / (size * size)

        @pl.when(p >= live_here)
        def _():
            amp_ref[p] = jnp.zeros((size, size), amp_ref.dtype)
            energy_ref[p] = 0.0

        return carry

    lax.fori_loop(0, pair_dev, second_step, 0)


def gather_kernel(
    row_count,
    col_count,
    blocks_ref,
    virtual_ref,
    occupied_ref,
    domains_ref,
    pairs_ref,
    weight_ref,
    all_ref,
    meta_ref,
    own,
    own_meta,
    local_sem,
    up_send,
    down_send,
    line_recv,
    side_send,
    side_recv,
    core_send,
    core_recv,
):
    row, col = lax.axis_index("row"), lax.axis_index("col")
    occ_dev, fit, size = blocks_ref.shape
    levels = row_count // 2
    z, x = row // 2, row % 2

    def device(line, side, core):
        return {"row": line * 2 + side, "col": core}

    below, above = z > 0, z < levels - 1
    barrier = pltpu.get_barrier_semaphore()

    def greet(target):
        pl.semaphore_signal(barrier, inc=1, device_id=target, device_id_type=pl.DeviceIdType.MESH)

    greet(device(z, 1 - x, col))
    greet(device(z, x, 1 - col))

    @pl.when(below)
    def _():
        greet(device(z - 1, x, col))

    @pl.when(above)
    def _():
        greet(device(z + 1, x, col))

    my_first = (row * col_count + col) * occ_dev
    r = lax.broadcasted_iota(jnp.int32, (FEAT, size), 0)
    for k in range(occ_dev):
        own[k, :size, :] = jnp.swapaxes(blocks_ref[k], 0, 1)
        v = virtual_ref[k : k + 1, :].astype(jnp.float32)
        o = occupied_ref[0:1, k : k + 1].astype(jnp.float32)
        dom = domains_ref[pl.ds(my_first + k, 1), :]
        high = (dom // 256).astype(jnp.float32)
        low = (dom % 256).astype(jnp.float32)
        rows = [v, 1.0, -o, 1.0, high, low, 1.0, 1.0]
        rows += [1.0, v, 1.0, -o, 256.0, 1.0, -256.0 * high, -low]
        out = jnp.zeros((FEAT, size), jnp.float32)
        for at, entry in enumerate(rows):
            out = jnp.where(r == at, entry, out)
        own[k, size:, :] = out.astype(own.dtype)
    slots = pairs_ref.shape[0]
    own_meta[...] = jnp.zeros_like(own_meta)
    own_meta[:slots, 0:2] = pairs_ref[...].astype(jnp.float32)
    own_meta[slots : slots + 1, 0:slots] = weight_ref[...]

    def index(line, side, core):
        return (line * 2 + side) * col_count + core

    me = index(z, x, col)
    keep = [
        pltpu.make_async_copy(own, all_ref.at[me], local_sem.at[0]),
        pltpu.make_async_copy(own_meta, meta_ref.at[me], local_sem.at[1]),
    ]
    for c in keep:
        c.start()
    neighbours = 2 + below.astype(jnp.int32) + above.astype(jnp.int32)
    pl.semaphore_wait(barrier, neighbours)

    def pair(slot, target, send, recv, at, mine=False):
        sources = (own, own_meta) if mine else (all_ref.at[slot], meta_ref.at[slot])
        return [
            pltpu.make_async_remote_copy(
                src_ref=sources[h],
                dst_ref=dst.at[slot],
                send_sem=send.at[at, h],
                recv_sem=recv.at[at, h],
                device_id=target,
                device_id_type=pl.DeviceIdType.MESH,
            )
            for h, dst in ((1, meta_ref), (0, all_ref))
        ]

    def start(copies):
        for c in copies:
            c.start()

    def sides(line, mine=False):
        start(pair(index(line, x, col), device(z, 1 - x, col), side_send, side_recv, line, mine))
        to_core(line, x, mine)

    def to_core(line, side, mine=False):
        at = line * 2 + side
        start(pair(index(line, side, col), device(z, x, 1 - col), core_send, core_recv, at, mine))

    def upward(line, mine=False):
        return pair(index(line, x, col), device(z + 1, x, col), up_send, line_recv, line, mine)

    def downward(line, mine=False):
        return pair(index(line, x, col), device(z - 1, x, col), down_send, line_recv, line, mine)

    def from_side(line):
        for c in pair(index(line, 1 - x, col), device(z, 1 - x, col), side_send, side_recv, line):
            c.wait_recv()
        to_core(line, 1 - x)

    @pl.when(above)
    def _():
        start(upward(z, True))

    @pl.when(below)
    def _():
        start(downward(z, True))

    sides(z, True)
    for s in range(1, levels):
        low, high = z - s, z + s

        @pl.when(low >= 0)
        def _():
            for c in upward(low):
                c.wait_recv()

            @pl.when(above)
            def _():
                start(upward(low))

            sides(low)

        @pl.when(high < levels)
        def _():
            for c in downward(high):
                c.wait_recv()

            @pl.when(below)
            def _():
                start(downward(high))

            sides(high)

        if s == 1:
            from_side(z)
        else:
            pl.when(z - (s - 1) >= 0)(lambda: from_side(z - (s - 1)))
            pl.when(z + (s - 1) < levels)(lambda: from_side(z + (s - 1)))
    last = levels - 1
    pl.when(z - last >= 0)(lambda: from_side(z - last))
    pl.when(z + last < levels)(lambda: from_side(z + last))
    for line in range(levels):
        for c in pair(index(line, x, col), device(z, 1 - x, col), side_send, side_recv, line):
            c.wait_send()
        for side in range(2):
            at = line * 2 + side
            slot = index(line, side, 1 - col)
            for c in pair(slot, device(z, x, 1 - col), core_send, core_recv, at):
                c.wait_recv()
                c.wait_send()

        @pl.when(above & (line <= z))
        def _():
            for c in upward(line):
                c.wait_send()

        @pl.when(below & (line >= z))
        def _():
            for c in downward(line):
                c.wait_send()

    for c in keep:
        c.wait()


def gather(blocks, virtual, occupied, domains, pair_list, coupling):
    row_count, col_count = lax.axis_size("row"), lax.axis_size("col")
    occ_dev, fit, size = blocks.shape
    slots = pair_list.shape[0]
    devices = row_count * col_count
    levels = row_count // 2
    vmem = pl.BlockSpec(memory_space=pltpu.VMEM)
    hbm = pl.BlockSpec(memory_space=pltpu.HBM)
    unit, meta = (occ_dev, size + FEAT, fit), (slots + 8, 128)
    sems = pltpu.SemaphoreType.DMA
    return pl.pallas_call(
        functools.partial(gather_kernel, row_count, col_count),
        out_shape=(
            jax.ShapeDtypeStruct((devices,) + unit, jnp.bfloat16),
            jax.ShapeDtypeStruct((devices,) + meta, jnp.float32),
        ),
        in_specs=[vmem] * 6,
        out_specs=(hbm, hbm),
        scratch_shapes=[
            pltpu.VMEM(unit, jnp.bfloat16),
            pltpu.VMEM(meta, jnp.float32),
            sems((2,)),
        ]
        + [sems((levels, 2))] * 5
        + [sems((row_count, 2))] * 2,
        compiler_params=pltpu.CompilerParams(
            collective_id=0, has_side_effects=True, vmem_limit_bytes=16 * 1024 * 1024
        ),
    )(blocks, virtual, occupied[None, :], domains, pair_list, coupling[None, :])


def shards(blocks, virtual, occupied, domains, pair_list, coupling):
    row_count, col_count = lax.axis_size("row"), lax.axis_size("col")
    occ_dev, fit, size = blocks.shape
    pair_dev = pair_list.shape[0]
    gathered, meta = gather(blocks, virtual, occupied, domains, pair_list, coupling)
    all_blocks = gathered.reshape((-1,) + gathered.shape[2:])
    pairs = meta[:, :pair_dev, :2].astype(jnp.int32)
    all_weight = meta[:, pair_dev, :pair_dev].reshape(-1)
    smem = pl.BlockSpec(memory_space=pltpu.SMEM)
    vmem = pl.BlockSpec(memory_space=pltpu.VMEM)
    items = max(row_count, col_count) * pair_dev + UNROLL
    return pl.pallas_call(
        functools.partial(pair_kernel, (row_count, col_count, occ_dev, pair_dev)),
        out_shape=(
            jax.ShapeDtypeStruct((pair_dev, size, size), jnp.bfloat16),
            jax.ShapeDtypeStruct((pair_dev,), jnp.float32),
        ),
        in_specs=[smem] * 3 + [vmem],
        out_specs=(vmem, smem),
        scratch_shapes=[
            pltpu.VMEM((pair_dev, size, size), jnp.float32),
            pltpu.VMEM((col_count * occ_dev, size, size), jnp.float32),
            pltpu.SMEM((row_count * col_count * occ_dev,), jnp.int32),
            pltpu.SMEM((items,), jnp.int32),
            pltpu.SMEM((items,), jnp.int32),
            pltpu.SMEM((items,), jnp.int32),
            pltpu.SMEM((items,), jnp.float32),
        ],
        compiler_params=pltpu.CompilerParams(vmem_limit_bytes=56 * 1024 * 1024),
    )(pairs[:, :, 0].reshape(-1), pairs[:, :, 1].reshape(-1), all_weight, all_blocks)


def solution(mesh):
    return jax.shard_map(
        shards,
        mesh=mesh,
        in_specs=(
            P(("grp", "row", "col"), None, None),
            P(("grp", "row", "col"), None),
            P(("grp", "row", "col")),
            P("grp", None),
            P(("grp", "row", "col"), None),
            P(("grp", "row", "col")),
        ),
        out_specs=(P(("grp", "row", "col"), None, None), P(("grp", "row", "col"))),
        check_vma=False,
    )
```

```python
import functools
import jax
import jax.numpy as jnp
from jax import lax
from jax.experimental import pallas as pl
from jax.experimental.pallas import tpu as pltpu
from jax.sharding import PartitionSpec as P

FEAT = 16
UNROLL = 4
PAIRS = 2
NT = (((1,), (1,)), ((), ()))
TN = (((0,), (0,)), ((), ()))
NN = (((1,), (0,)), ((), ()))


def mm(a, b, dims):
    return lax.dot_general(a, b, dims, preferred_element_type=jnp.float32)


def pair_kernel(
    dims,
    first_ref,
    second_ref,
    weight_ref,
    gathered_ref,
    amp_ref,
    energy_ref,
    blocks_ref,
    sums,
    mixes,
    slot_of,
    centre,
    count,
    item_o,
    item_w,
    load_sem,
):
    row_count, col_count, occ_dev, pair_dev = dims
    my_row, my_col = lax.axis_index("row"), lax.axis_index("col")
    orbitals = row_count * col_count * occ_dev
    near = col_count * occ_dev
    size = amp_ref.shape[1]
    cap = item_o.shape[1]
    mine = (my_row * col_count + my_col) * pair_dev
    near_base = my_row * near
    load = pltpu.make_async_copy(gathered_ref, blocks_ref, load_sem)
    load.start()

    def clear(j, carry):
        slot_of[j] = -1
        return carry

    lax.fori_loop(0, orbitals, clear, 0)
    for k in range(near):
        centre[k] = near_base + k
    for k in range(near + pair_dev):
        count[k] = 0

    def claim(p, used):
        live = first_ref[mine + p] >= 0
        j = jnp.maximum(second_ref[mine + p], 0)
        fresh = live & (slot_of[j] < 0)

        @pl.when(fresh)
        def _():
            slot_of[j] = used
            centre[used] = j

        return used + fresh.astype(jnp.int32)

    used = lax.fori_loop(0, pair_dev, claim, jnp.int32(near))

    def add(slot, orbital, w):
        n = count[slot]
        item_o[slot, n] = orbital
        item_w[slot, n] = -w
        count[slot] = n + 1

    def col_items(owner, carry):
        def step(q, carry):
            at = (owner * col_count + my_col) * pair_dev + q
            i = first_ref[at]
            slot = slot_of[jnp.maximum(second_ref[at], 0)]

            @pl.when((i >= 0) & (slot >= 0))
            def _():
                add(slot, i, weight_ref[at])

            return carry

        return lax.fori_loop(0, pair_dev, step, carry)

    lax.fori_loop(0, row_count, col_items, 0)

    def row_items(q, carry):
        at = my_row * col_count * pair_dev + q
        i = first_ref[at]

        @pl.when(i >= 0)
        def _():
            add(i - near_base, second_ref[at], weight_ref[at])

        return carry

    lax.fori_loop(0, col_count * pair_dev, row_items, 0)

    def pad(slot, carry):
        n = count[slot]
        for u in range(UNROLL):
            item_o[slot, n + u] = 0
            item_w[slot, n + u] = 0.0
        return carry

    lax.fori_loop(0, used, pad, 0)
    load.wait()

    def block(o):
        return blocks_ref[o, :size, :]

    def features(o):
        f = blocks_ref[o, size:, :].astype(jnp.float32)
        left, right = f[:8], f[8:]
        top = lax.broadcasted_iota(jnp.int32, left.shape, 0) < 4
        halves = jnp.where(top, right, 0.0), jnp.where(top, 0.0, right)
        return left.astype(jnp.bfloat16), *(h.astype(jnp.bfloat16) for h in halves)

    def hits(gap):
        return jnp.where(gap == 0.0, 1.0, 0.0).astype(jnp.bfloat16)

    def one_centre(slot, carry):
        o = centre[slot]
        sums[...] = jnp.zeros_like(sums)

        def step(t, carry):
            turned = block(o).T
            left_o, diff_o, _ = features(o)
            others = [item_o[slot, t * UNROLL + u] for u in range(UNROLL)]
            weights = [item_w[slot, t * UNROLL + u] for u in range(UNROLL)]
            feats = [features(n) for n in others]
            gap = mm(left_o, jnp.concatenate([f[2] for f in feats], axis=1), TN)
            scaled = []
            for n, w, f in zip(others, weights, feats):
                integ = mm(block(n), turned, NN)
                denom = mm(f[0], diff_o, TN)
                amp = (integ * w) * pl.reciprocal(denom, approx=True)
                scaled.append(amp.astype(jnp.bfloat16))
            sums[...] += mm(hits(gap), jnp.concatenate(scaled, axis=0), NN)
            return carry

        lax.fori_loop(0, (count[slot] + UNROLL - 1) // UNROLL, step, 0)
        mixes[slot] = sums[...].astype(jnp.bfloat16)
        return carry

    lax.fori_loop(0, used, one_centre, 0)
    for k in range(near):
        mixes[k] = mixes[k].T

    def one_pair(p):
        live = first_ref[mine + p] >= 0
        i = jnp.where(live, first_ref[mine + p], near_base)
        j = jnp.maximum(second_ref[mine + p], 0)
        integ = mm(block(i), block(j), NT)
        left_i, diff_i, gap_i = features(i)
        left_j, diff_j, gap_j = features(j)
        denom = mm(left_i, diff_j, TN)
        match = hits(mm(left_i, gap_j, TN))
        col_mix = mixes[jnp.maximum(slot_of[j], 0)]
        row_mix = mixes[i - near_base]
        both = jnp.concatenate([match, row_mix], axis=1)
        mixed = mm(both, jnp.concatenate([col_mix, match], axis=0), NN)
        amp = (mixed - integ) * pl.reciprocal(denom, approx=True)
        amp = jnp.where(live, amp, 0.0)
        amp_ref[p] = amp.astype(amp_ref.dtype)
        energy_ref[p] = jnp.sum(integ * amp) / (size * size)

    def second_step(t, carry):
        @pl.when(first_ref[mine + t * PAIRS] >= 0)
        def _():
            for u in range(PAIRS):
                one_pair(t * PAIRS + u)

        @pl.when(first_ref[mine + t * PAIRS] < 0)
        def _():
            for u in range(PAIRS):
                amp_ref[t * PAIRS + u] = jnp.zeros((size, size), amp_ref.dtype)
                energy_ref[t * PAIRS + u] = 0.0

        return carry

    lax.fori_loop(0, pair_dev // PAIRS, second_step, 0)


def gather_kernel(
    row_count,
    col_count,
    blocks_ref,
    virtual_ref,
    occupied_ref,
    domains_ref,
    pairs_ref,
    weight_ref,
    all_ref,
    meta_ref,
    own,
    own_meta,
    blocks_in,
    virtual_in,
    occupied_in,
    domains_in,
    pairs_in,
    weight_in,
    local_sem,
    load_sem,
    up_send,
    down_send,
    line_recv,
    side_send,
    side_recv,
    core_send,
    core_recv,
):
    row, col = lax.axis_index("row"), lax.axis_index("col")
    sources = (blocks_ref, virtual_ref, occupied_ref, domains_ref, pairs_ref, weight_ref)
    held = (blocks_in, virtual_in, occupied_in, domains_in, pairs_in, weight_in)
    loads = [
        pltpu.make_async_copy(src, dst, load_sem.at[k])
        for k, (src, dst) in enumerate(zip(sources, held))
    ]
    for c in loads:
        c.start()
    blocks_ref, virtual_ref, occupied_ref, domains_ref, pairs_ref, weight_ref = held
    occ_dev, fit, size = blocks_ref.shape
    levels = row_count // 2
    z, x = row // 2, row % 2

    def device(line, side, core):
        return {"row": line * 2 + side, "col": core}

    below, above = z > 0, z < levels - 1
    barrier = pltpu.get_barrier_semaphore()

    def greet(target):
        pl.semaphore_signal(barrier, inc=1, device_id=target, device_id_type=pl.DeviceIdType.MESH)

    greet(device(z, 1 - x, col))
    greet(device(z, x, 1 - col))

    @pl.when(below)
    def _():
        greet(device(z - 1, x, col))

    @pl.when(above)
    def _():
        greet(device(z + 1, x, col))

    for c in loads:
        c.wait()
    my_first = (row * col_count + col) * occ_dev
    r = lax.broadcasted_iota(jnp.int32, (FEAT, size), 0)
    for k in range(occ_dev):
        own[k, :size, :] = jnp.swapaxes(blocks_ref[k], 0, 1)
        v = virtual_ref[k : k + 1, :].astype(jnp.float32)
        o = occupied_ref[0:1, k : k + 1].astype(jnp.float32)
        dom = domains_ref[pl.ds(my_first + k, 1), :]
        high = (dom // 256).astype(jnp.float32)
        low = (dom % 256).astype(jnp.float32)
        rows = [v, 1.0, -o, 1.0, high, low, 1.0, 1.0]
        rows += [1.0, v, 1.0, -o, 256.0, 1.0, -256.0 * high, -low]
        out = jnp.zeros((FEAT, size), jnp.float32)
        for at, entry in enumerate(rows):
            out = jnp.where(r == at, entry, out)
        own[k, size:, :] = out.astype(own.dtype)
    slots = pairs_ref.shape[0]
    own_meta[...] = jnp.zeros_like(own_meta)
    own_meta[:slots, 0:2] = pairs_ref[...].astype(jnp.float32)
    own_meta[slots : slots + 1, 0:slots] = weight_ref[...]

    def index(line, side, core):
        return (line * 2 + side) * col_count + core

    me = index(z, x, col)
    keep = [
        pltpu.make_async_copy(own, all_ref.at[me], local_sem.at[0]),
        pltpu.make_async_copy(own_meta, meta_ref.at[me], local_sem.at[1]),
    ]
    for c in keep:
        c.start()
    neighbours = 2 + below.astype(jnp.int32) + above.astype(jnp.int32)
    pl.semaphore_wait(barrier, neighbours)

    def pair(slot, target, send, recv, at, mine=False):
        sources = (own, own_meta) if mine else (all_ref.at[slot], meta_ref.at[slot])
        return [
            pltpu.make_async_remote_copy(
                src_ref=sources[h],
                dst_ref=dst.at[slot],
                send_sem=send.at[at, h],
                recv_sem=recv.at[at, h],
                device_id=target,
                device_id_type=pl.DeviceIdType.MESH,
            )
            for h, dst in ((1, meta_ref), (0, all_ref))
        ]

    def start(copies):
        for c in copies:
            c.start()

    def sides(line, mine=False):
        start(pair(index(line, x, col), device(z, 1 - x, col), side_send, side_recv, line, mine))
        to_core(line, x, mine)

    def to_core(line, side, mine=False):
        at = line * 2 + side
        start(pair(index(line, side, col), device(z, x, 1 - col), core_send, core_recv, at, mine))

    def upward(line, mine=False):
        return pair(index(line, x, col), device(z + 1, x, col), up_send, line_recv, line, mine)

    def downward(line, mine=False):
        return pair(index(line, x, col), device(z - 1, x, col), down_send, line_recv, line, mine)

    def from_side(line):
        for c in pair(index(line, 1 - x, col), device(z, 1 - x, col), side_send, side_recv, line):
            c.wait_recv()
        to_core(line, 1 - x)

    @pl.when(above)
    def _():
        start(upward(z, True))

    @pl.when(below)
    def _():
        start(downward(z, True))

    sides(z, True)
    for s in range(1, levels):
        low, high = z - s, z + s

        @pl.when(low >= 0)
        def _():
            for c in upward(low):
                c.wait_recv()

            @pl.when(above)
            def _():
                start(upward(low))

            sides(low)

        @pl.when(high < levels)
        def _():
            for c in downward(high):
                c.wait_recv()

            @pl.when(below)
            def _():
                start(downward(high))

            sides(high)

        if s == 1:
            from_side(z)
        else:
            pl.when(z - (s - 1) >= 0)(lambda: from_side(z - (s - 1)))
            pl.when(z + (s - 1) < levels)(lambda: from_side(z + (s - 1)))
    last = levels - 1
    pl.when(z - last >= 0)(lambda: from_side(z - last))
    pl.when(z + last < levels)(lambda: from_side(z + last))
    for line in range(levels):
        for c in pair(index(line, x, col), device(z, 1 - x, col), side_send, side_recv, line):
            c.wait_send()
        for side in range(2):
            at = line * 2 + side
            slot = index(line, side, 1 - col)
            for c in pair(slot, device(z, x, 1 - col), core_send, core_recv, at):
                c.wait_recv()
                c.wait_send()

        @pl.when(above & (line <= z))
        def _():
            for c in upward(line):
                c.wait_send()

        @pl.when(below & (line >= z))
        def _():
            for c in downward(line):
                c.wait_send()

    for c in keep:
        c.wait()


def gather(blocks, virtual, occupied, domains, pair_list, coupling):
    row_count, col_count = lax.axis_size("row"), lax.axis_size("col")
    occ_dev, fit, size = blocks.shape
    slots = pair_list.shape[0]
    devices = row_count * col_count
    levels = row_count // 2
    hbm = pl.BlockSpec(memory_space=pltpu.HBM)
    arguments = (blocks, virtual, occupied[None, :], domains, pair_list, coupling[None, :])
    unit, meta = (occ_dev, size + FEAT, fit), (slots + 8, 128)
    sems = pltpu.SemaphoreType.DMA
    return pl.pallas_call(
        functools.partial(gather_kernel, row_count, col_count),
        out_shape=(
            jax.ShapeDtypeStruct((devices,) + unit, jnp.bfloat16),
            jax.ShapeDtypeStruct((devices,) + meta, jnp.float32),
        ),
        in_specs=[hbm] * 6,
        out_specs=(hbm, hbm),
        scratch_shapes=[
            pltpu.VMEM(unit, jnp.bfloat16),
            pltpu.VMEM(meta, jnp.float32),
        ]
        + [pltpu.VMEM(a.shape, a.dtype) for a in arguments]
        + [sems((2,)), sems((6,))]
        + [sems((levels, 2))] * 5
        + [sems((row_count, 2))] * 2,
        compiler_params=pltpu.CompilerParams(
            collective_id=0, has_side_effects=True, vmem_limit_bytes=16 * 1024 * 1024
        ),
    )(*arguments)


def shards(blocks, virtual, occupied, domains, pair_list, coupling):
    row_count, col_count = lax.axis_size("row"), lax.axis_size("col")
    occ_dev, fit, size = blocks.shape
    pair_dev = pair_list.shape[0]
    gathered, meta = gather(blocks, virtual, occupied, domains, pair_list, coupling)
    all_blocks = gathered.reshape((-1,) + gathered.shape[2:])
    pairs = meta[:, :pair_dev, :2].astype(jnp.int32)
    all_weight = meta[:, pair_dev, :pair_dev].reshape(-1)
    smem = pl.BlockSpec(memory_space=pltpu.SMEM)
    vmem = pl.BlockSpec(memory_space=pltpu.VMEM)
    near = col_count * occ_dev
    cap = max(near * row_count, col_count * pair_dev) + UNROLL
    return pl.pallas_call(
        functools.partial(pair_kernel, (row_count, col_count, occ_dev, pair_dev)),
        out_shape=(
            jax.ShapeDtypeStruct((pair_dev, size, size), jnp.bfloat16),
            jax.ShapeDtypeStruct((pair_dev,), jnp.float32),
        ),
        in_specs=[smem] * 3 + [pl.BlockSpec(memory_space=pltpu.HBM)],
        out_specs=(vmem, smem),
        scratch_shapes=[
            pltpu.VMEM(all_blocks.shape, jnp.bfloat16),
            pltpu.VMEM((size, size), jnp.float32),
            pltpu.VMEM((near + pair_dev, size, size), jnp.bfloat16),
            pltpu.SMEM((row_count * near,), jnp.int32),
            pltpu.SMEM((near + pair_dev,), jnp.int32),
            pltpu.SMEM((near + pair_dev,), jnp.int32),
            pltpu.SMEM((near + pair_dev, cap), jnp.int32),
            pltpu.SMEM((near + pair_dev, cap), jnp.float32),
            pltpu.SemaphoreType.DMA,
        ],
        compiler_params=pltpu.CompilerParams(vmem_limit_bytes=56 * 1024 * 1024),
    )(pairs[:, :, 0].reshape(-1), pairs[:, :, 1].reshape(-1), all_weight, all_blocks)


def solution(mesh):
    return jax.shard_map(
        shards,
        mesh=mesh,
        in_specs=(
            P(("grp", "row", "col"), None, None),
            P(("grp", "row", "col"), None),
            P(("grp", "row", "col")),
            P("grp", None),
            P(("grp", "row", "col"), None),
            P(("grp", "row", "col")),
        ),
        out_specs=(P(("grp", "row", "col"), None, None), P(("grp", "row", "col"))),
        check_vma=False,
    )
```

```python
import functools
import jax
import jax.numpy as jnp
from jax import lax
from jax.experimental import pallas as pl
from jax.experimental.pallas import tpu as pltpu
from jax.sharding import PartitionSpec as P

FEAT = 16
UNROLL = 4
PAIRS = 2
LANES = 128
NT = (((1,), (1,)), ((), ()))
NN = (((1,), (0,)), ((), ()))


def mm(a, b, dims):
    return lax.dot_general(a, b, dims, preferred_element_type=jnp.float32)


def pair_kernel(
    dims,
    first_ref,
    second_ref,
    weight_ref,
    gathered_ref,
    amp_ref,
    energy_ref,
    blocks_ref,
    sums,
    mixes,
    turned,
    energy_cols,
    domain_cols,
    slot_of,
    centre,
    count,
    item_o,
    item_w,
    load_sem,
):
    row_count, col_count, occ_dev, pair_dev = dims
    my_row, my_col = lax.axis_index("row"), lax.axis_index("col")
    orbitals = row_count * col_count * occ_dev
    near = col_count * occ_dev
    size = amp_ref.shape[1]
    cap = item_o.shape[1]
    mine = (my_row * col_count + my_col) * pair_dev
    near_base = my_row * near
    load = pltpu.make_async_copy(gathered_ref, blocks_ref, load_sem)
    load.start()

    def clear(j, carry):
        slot_of[j] = -1
        return carry

    lax.fori_loop(0, orbitals, clear, 0)
    for k in range(near):
        centre[k] = near_base + k
    for k in range(near + pair_dev):
        count[k] = 0

    def claim(p, used):
        live = first_ref[mine + p] >= 0
        j = jnp.maximum(second_ref[mine + p], 0)
        fresh = live & (slot_of[j] < 0)

        @pl.when(fresh)
        def _():
            slot_of[j] = used
            centre[used] = j

        return used + fresh.astype(jnp.int32)

    used = lax.fori_loop(0, pair_dev, claim, jnp.int32(near))

    def add(slot, orbital, w):
        n = count[slot]
        item_o[slot, n] = orbital
        item_w[slot, n] = -w
        count[slot] = n + 1

    def col_items(owner, carry):
        def step(q, carry):
            at = (owner * col_count + my_col) * pair_dev + q
            i = first_ref[at]
            slot = slot_of[jnp.maximum(second_ref[at], 0)]

            @pl.when((i >= 0) & (slot >= 0))
            def _():
                add(slot, i, weight_ref[at])

            return carry

        return lax.fori_loop(0, pair_dev, step, carry)

    lax.fori_loop(0, row_count, col_items, 0)

    def row_items(q, carry):
        at = my_row * col_count * pair_dev + q
        i = first_ref[at]

        @pl.when(i >= 0)
        def _():
            add(i - near_base, second_ref[at], weight_ref[at])

        return carry

    lax.fori_loop(0, col_count * pair_dev, row_items, 0)

    def pad(slot, carry):
        n = count[slot]
        for u in range(UNROLL):
            item_o[slot, n + u] = 0
            item_w[slot, n + u] = 0.0
        return carry

    lax.fori_loop(0, used, pad, 0)
    load.wait()

    def block(o):
        return blocks_ref[o, :size, :]

    def rows(o):
        f = blocks_ref[o, size:, :].astype(jnp.float32)
        return f[9:10], f[11:12], -(f[14:15] + f[15:16])

    def column(row):
        return jnp.broadcast_to(row, (LANES, size)).T

    def wide(col):
        return jnp.concatenate([col.astype(jnp.float32)] * (size // LANES), axis=1)

    def hits(col, row):
        return jnp.where(col == row, 1.0, 0.0).astype(jnp.bfloat16)

    def spread(o, carry):
        energy_cols[o] = column(rows(o)[0]).astype(jnp.bfloat16)
        return carry

    lax.fori_loop(0, orbitals, spread, 0)

    def one_centre(slot, carry):
        o = centre[slot]
        sums[...] = jnp.zeros_like(sums)
        turned[...] = block(o).T
        v, minus, domain = rows(o)
        kept = jnp.minimum(slot, near)
        domain_cols[kept] = column(domain)

        def step(t, carry):
            others = [item_o[slot, t * UNROLL + u] for u in range(UNROLL)]
            weights = [item_w[slot, t * UNROLL + u] for u in range(UNROLL)]
            matches, scaled = [], []
            for n, w in zip(others, weights):
                _, minus_n, domain_n = rows(n)
                integ = mm(block(n), turned[...], NN)
                denom = wide(energy_cols[n]) + (v + minus + minus_n)
                amp = (integ * w) * pl.reciprocal(denom, approx=True)
                scaled.append(amp.astype(jnp.bfloat16))
                matches.append(hits(wide(domain_cols[kept]), domain_n))
            match = jnp.concatenate(matches, axis=1)
            sums[...] += mm(match, jnp.concatenate(scaled, axis=0), NN)
            return carry

        lax.fori_loop(0, (count[slot] + UNROLL - 1) // UNROLL, step, 0)
        mixes[slot] = sums[...].astype(jnp.bfloat16)
        return carry

    lax.fori_loop(0, used, one_centre, 0)
    for k in range(near):
        mixes[k] = mixes[k].T

    def one_pair(p):
        live = first_ref[mine + p] >= 0
        i = jnp.where(live, first_ref[mine + p], near_base)
        j = jnp.maximum(second_ref[mine + p], 0)
        integ = mm(block(i), block(j), NT)
        v, minus, domain = rows(j)
        denom = wide(energy_cols[i]) + (v + minus + rows(i)[1])
        match = hits(wide(domain_cols[i - near_base]), domain)
        col_mix = mixes[jnp.maximum(slot_of[j], 0)]
        row_mix = mixes[i - near_base]
        both = jnp.concatenate([match, row_mix], axis=1)
        mixed = mm(both, jnp.concatenate([col_mix, match], axis=0), NN)
        amp = (mixed - integ) * pl.reciprocal(denom, approx=True)
        amp = jnp.where(live, amp, 0.0)
        amp_ref[p] = amp.astype(amp_ref.dtype)
        energy_ref[p] = jnp.sum(integ * amp) / (size * size)

    def second_step(t, carry):
        @pl.when(first_ref[mine + t * PAIRS] >= 0)
        def _():
            for u in range(PAIRS):
                one_pair(t * PAIRS + u)

        @pl.when(first_ref[mine + t * PAIRS] < 0)
        def _():
            for u in range(PAIRS):
                amp_ref[t * PAIRS + u] = jnp.zeros((size, size), amp_ref.dtype)
                energy_ref[t * PAIRS + u] = 0.0

        return carry

    lax.fori_loop(0, pair_dev // PAIRS, second_step, 0)


def gather_kernel(
    row_count,
    col_count,
    blocks_ref,
    virtual_ref,
    occupied_ref,
    domains_ref,
    pairs_ref,
    weight_ref,
    all_ref,
    meta_ref,
    own,
    own_meta,
    blocks_in,
    virtual_in,
    occupied_in,
    domains_in,
    pairs_in,
    weight_in,
    local_sem,
    load_sem,
    up_send,
    down_send,
    line_recv,
    side_send,
    side_recv,
    core_send,
    core_recv,
):
    row, col = lax.axis_index("row"), lax.axis_index("col")
    sources = (blocks_ref, virtual_ref, occupied_ref, domains_ref, pairs_ref, weight_ref)
    held = (blocks_in, virtual_in, occupied_in, domains_in, pairs_in, weight_in)
    loads = [
        pltpu.make_async_copy(src, dst, load_sem.at[k])
        for k, (src, dst) in enumerate(zip(sources, held))
    ]
    for c in loads:
        c.start()
    blocks_ref, virtual_ref, occupied_ref, domains_ref, pairs_ref, weight_ref = held
    occ_dev, fit, size = blocks_ref.shape
    levels = row_count // 2
    z, x = row // 2, row % 2

    def device(line, side, core):
        return {"row": line * 2 + side, "col": core}

    below, above = z > 0, z < levels - 1
    barrier = pltpu.get_barrier_semaphore()

    def greet(target):
        pl.semaphore_signal(barrier, inc=1, device_id=target, device_id_type=pl.DeviceIdType.MESH)

    greet(device(z, 1 - x, col))
    greet(device(z, x, 1 - col))

    @pl.when(below)
    def _():
        greet(device(z - 1, x, col))

    @pl.when(above)
    def _():
        greet(device(z + 1, x, col))

    for c in loads:
        c.wait()
    my_first = (row * col_count + col) * occ_dev
    r = lax.broadcasted_iota(jnp.int32, (FEAT, size), 0)
    for k in range(occ_dev):
        own[k, :size, :] = jnp.swapaxes(blocks_ref[k], 0, 1)
        v = virtual_ref[k : k + 1, :].astype(jnp.float32)
        o = occupied_ref[0:1, k : k + 1].astype(jnp.float32)
        dom = domains_ref[pl.ds(my_first + k, 1), :]
        high = (dom // 256).astype(jnp.float32)
        low = (dom % 256).astype(jnp.float32)
        rows = [v, 1.0, -o, 1.0, high, low, 1.0, 1.0]
        rows += [1.0, v, 1.0, -o, 256.0, 1.0, -256.0 * high, -low]
        out = jnp.zeros((FEAT, size), jnp.float32)
        for at, entry in enumerate(rows):
            out = jnp.where(r == at, entry, out)
        own[k, size:, :] = out.astype(own.dtype)
    slots = pairs_ref.shape[0]
    own_meta[...] = jnp.zeros_like(own_meta)
    own_meta[:slots, 0:2] = pairs_ref[...].astype(jnp.float32)
    own_meta[slots : slots + 1, 0:slots] = weight_ref[...]

    def index(line, side, core):
        return (line * 2 + side) * col_count + core

    me = index(z, x, col)
    keep = [
        pltpu.make_async_copy(own, all_ref.at[me], local_sem.at[0]),
        pltpu.make_async_copy(own_meta, meta_ref.at[me], local_sem.at[1]),
    ]
    for c in keep:
        c.start()
    neighbours = 2 + below.astype(jnp.int32) + above.astype(jnp.int32)
    pl.semaphore_wait(barrier, neighbours)

    def pair(slot, target, send, recv, at, mine=False):
        sources = (own, own_meta) if mine else (all_ref.at[slot], meta_ref.at[slot])
        return [
            pltpu.make_async_remote_copy(
                src_ref=sources[h],
                dst_ref=dst.at[slot],
                send_sem=send.at[at, h],
                recv_sem=recv.at[at, h],
                device_id=target,
                device_id_type=pl.DeviceIdType.MESH,
            )
            for h, dst in ((1, meta_ref), (0, all_ref))
        ]

    def start(copies):
        for c in copies:
            c.start()

    def sides(line, mine=False):
        start(pair(index(line, x, col), device(z, 1 - x, col), side_send, side_recv, line, mine))
        to_core(line, x, mine)

    def to_core(line, side, mine=False):
        at = line * 2 + side
        start(pair(index(line, side, col), device(z, x, 1 - col), core_send, core_recv, at, mine))

    def upward(line, mine=False):
        return pair(index(line, x, col), device(z + 1, x, col), up_send, line_recv, line, mine)

    def downward(line, mine=False):
        return pair(index(line, x, col), device(z - 1, x, col), down_send, line_recv, line, mine)

    def from_side(line):
        for c in pair(index(line, 1 - x, col), device(z, 1 - x, col), side_send, side_recv, line):
            c.wait_recv()
        to_core(line, 1 - x)

    @pl.when(above)
    def _():
        start(upward(z, True))

    @pl.when(below)
    def _():
        start(downward(z, True))

    sides(z, True)
    for s in range(1, levels):
        low, high = z - s, z + s

        @pl.when(low >= 0)
        def _():
            for c in upward(low):
                c.wait_recv()

            @pl.when(above)
            def _():
                start(upward(low))

            sides(low)

        @pl.when(high < levels)
        def _():
            for c in downward(high):
                c.wait_recv()

            @pl.when(below)
            def _():
                start(downward(high))

            sides(high)

        if s == 1:
            from_side(z)
        else:
            pl.when(z - (s - 1) >= 0)(lambda: from_side(z - (s - 1)))
            pl.when(z + (s - 1) < levels)(lambda: from_side(z + (s - 1)))
    last = levels - 1
    pl.when(z - last >= 0)(lambda: from_side(z - last))
    pl.when(z + last < levels)(lambda: from_side(z + last))
    for line in range(levels):
        for c in pair(index(line, x, col), device(z, 1 - x, col), side_send, side_recv, line):
            c.wait_send()
        for side in range(2):
            at = line * 2 + side
            slot = index(line, side, 1 - col)
            for c in pair(slot, device(z, x, 1 - col), core_send, core_recv, at):
                c.wait_recv()
                c.wait_send()

        @pl.when(above & (line <= z))
        def _():
            for c in upward(line):
                c.wait_send()

        @pl.when(below & (line >= z))
        def _():
            for c in downward(line):
                c.wait_send()

    for c in keep:
        c.wait()


def gather(blocks, virtual, occupied, domains, pair_list, coupling):
    row_count, col_count = lax.axis_size("row"), lax.axis_size("col")
    occ_dev, fit, size = blocks.shape
    slots = pair_list.shape[0]
    devices = row_count * col_count
    levels = row_count // 2
    hbm = pl.BlockSpec(memory_space=pltpu.HBM)
    arguments = (blocks, virtual, occupied[None, :], domains, pair_list, coupling[None, :])
    unit, meta = (occ_dev, size + FEAT, fit), (slots + 8, 128)
    sems = pltpu.SemaphoreType.DMA
    return pl.pallas_call(
        functools.partial(gather_kernel, row_count, col_count),
        out_shape=(
            jax.ShapeDtypeStruct((devices,) + unit, jnp.bfloat16),
            jax.ShapeDtypeStruct((devices,) + meta, jnp.float32),
        ),
        in_specs=[hbm] * 6,
        out_specs=(hbm, hbm),
        scratch_shapes=[
            pltpu.VMEM(unit, jnp.bfloat16),
            pltpu.VMEM(meta, jnp.float32),
        ]
        + [pltpu.VMEM(a.shape, a.dtype) for a in arguments]
        + [sems((2,)), sems((6,))]
        + [sems((levels, 2))] * 5
        + [sems((row_count, 2))] * 2,
        compiler_params=pltpu.CompilerParams(
            collective_id=0, has_side_effects=True, vmem_limit_bytes=60 * 1024 * 1024
        ),
    )(*arguments)


def shards(blocks, virtual, occupied, domains, pair_list, coupling):
    row_count, col_count = lax.axis_size("row"), lax.axis_size("col")
    occ_dev, fit, size = blocks.shape
    pair_dev = pair_list.shape[0]
    gathered, meta = gather(blocks, virtual, occupied, domains, pair_list, coupling)
    all_blocks = gathered.reshape((-1,) + gathered.shape[2:])
    pairs = meta[:, :pair_dev, :2].astype(jnp.int32)
    all_weight = meta[:, pair_dev, :pair_dev].reshape(-1)
    smem = pl.BlockSpec(memory_space=pltpu.SMEM)
    vmem = pl.BlockSpec(memory_space=pltpu.VMEM)
    near = col_count * occ_dev
    cap = max(near * row_count, col_count * pair_dev) + UNROLL
    return pl.pallas_call(
        functools.partial(pair_kernel, (row_count, col_count, occ_dev, pair_dev)),
        out_shape=(
            jax.ShapeDtypeStruct((pair_dev, size, size), jnp.bfloat16),
            jax.ShapeDtypeStruct((pair_dev,), jnp.float32),
        ),
        in_specs=[smem] * 3 + [pl.BlockSpec(memory_space=pltpu.HBM)],
        out_specs=(vmem, smem),
        scratch_shapes=[
            pltpu.VMEM(all_blocks.shape, jnp.bfloat16),
            pltpu.VMEM((size, size), jnp.float32),
            pltpu.VMEM((near + pair_dev, size, size), jnp.bfloat16),
            pltpu.VMEM((fit, size), jnp.bfloat16),
            pltpu.VMEM((row_count * near, size, LANES), jnp.bfloat16),
            pltpu.VMEM((near + 1, size, LANES), jnp.float32),
            pltpu.SMEM((row_count * near,), jnp.int32),
            pltpu.SMEM((near + pair_dev,), jnp.int32),
            pltpu.SMEM((near + pair_dev,), jnp.int32),
            pltpu.SMEM((near + pair_dev, cap), jnp.int32),
            pltpu.SMEM((near + pair_dev, cap), jnp.float32),
            pltpu.SemaphoreType.DMA,
        ],
        compiler_params=pltpu.CompilerParams(vmem_limit_bytes=60 * 1024 * 1024),
    )(pairs[:, :, 0].reshape(-1), pairs[:, :, 1].reshape(-1), all_weight, all_blocks)


def solution(mesh):
    return jax.shard_map(
        shards,
        mesh=mesh,
        in_specs=(
            P(("grp", "row", "col"), None, None),
            P(("grp", "row", "col"), None),
            P(("grp", "row", "col")),
            P("grp", None),
            P(("grp", "row", "col"), None),
            P(("grp", "row", "col")),
        ),
        out_specs=(P(("grp", "row", "col"), None, None), P(("grp", "row", "col"))),
        check_vma=False,
    )
```

```python
import functools
import jax
import jax.numpy as jnp
from jax import lax
from jax.experimental import pallas as pl
from jax.experimental.pallas import tpu as pltpu
from jax.sharding import PartitionSpec as P

FEAT = 16
UNROLL = 4
PAIRS = 4
LANES = 128
NT = (((1,), (1,)), ((), ()))
NN = (((1,), (0,)), ((), ()))


def mm(a, b, dims):
    return lax.dot_general(a, b, dims, preferred_element_type=jnp.float32)


def pair_kernel(
    dims,
    meta_ref,
    gathered_ref,
    amp_ref,
    energy_ref,
    blocks_ref,
    sums,
    mixes,
    turned,
    energy_cols,
    domain_cols,
    slot_of,
    centre,
    count,
    item_o,
    item_w,
    meta,
    load_sem,
    meta_sem,
):
    row_count, col_count, occ_dev, pair_dev = dims
    my_row, my_col = lax.axis_index("row"), lax.axis_index("col")
    orbitals = row_count * col_count * occ_dev
    near = col_count * occ_dev
    size = amp_ref.shape[1]
    cap = item_o.shape[1]
    near_base = my_row * near
    load = pltpu.make_async_copy(gathered_ref, blocks_ref, load_sem)
    load.start()
    fetch = pltpu.make_async_copy(meta_ref, meta, meta_sem)
    fetch.start()
    trash = near + pair_dev

    def clear(j, carry):
        slot_of[j] = -1
        return carry

    lax.fori_loop(0, orbitals, clear, 0)
    for k in range(near):
        centre[k] = near_base + k
    for k in range(near + pair_dev + 1):
        count[k] = 0
    fetch.wait()
    me = my_row * col_count + my_col

    def entry(row, device, q):
        return meta[device, row, q].astype(jnp.int32)

    used = jnp.int32(near)
    for p in range(pair_dev):
        live = entry(0, me, p) >= 0
        j = jnp.maximum(entry(1, me, p), 0)
        known = slot_of[j]
        fresh = live & (known < 0)
        slot_of[j] = jnp.where(fresh, used, known)
        centre[jnp.where(fresh, used, trash)] = j
        used = used + fresh.astype(jnp.int32)

    def add(take, slot, orbital, w):
        slot = jnp.where(take, slot, trash)
        n = count[slot]
        item_o[slot, n] = orbital
        item_w[slot, n] = -w
        count[slot] = n + take.astype(jnp.int32)

    def col_items(owner, carry):
        device = owner * col_count + my_col
        for q in range(pair_dev):
            i = entry(0, device, q)
            slot = slot_of[jnp.maximum(entry(1, device, q), 0)]
            add((i >= 0) & (slot >= 0), slot, i, meta[device, 2, q])
        return carry

    lax.fori_loop(0, row_count, col_items, 0)

    def row_items(side, carry):
        device = my_row * col_count + side
        for q in range(pair_dev):
            i = entry(0, device, q)
            add(i >= 0, i - near_base, entry(1, device, q), meta[device, 2, q])
        return carry

    lax.fori_loop(0, col_count, row_items, 0)

    def pad(slot, carry):
        n = count[slot]
        for u in range(UNROLL):
            item_o[slot, n + u] = 0
            item_w[slot, n + u] = 0.0
        return carry

    lax.fori_loop(0, used, pad, 0)
    load.wait()

    def block(o):
        return blocks_ref[o, :size, :]

    def rows(o):
        f = blocks_ref[o, size:, :].astype(jnp.float32)
        return f[9:10], f[11:12], -(f[14:15] + f[15:16])

    def column(row):
        return jnp.broadcast_to(row, (LANES, size)).T

    def wide(col):
        return jnp.concatenate([col.astype(jnp.float32)] * (size // LANES), axis=1)

    def hits(col, row):
        return jnp.where(col == row, 1.0, 0.0).astype(jnp.bfloat16)

    def spread(o, carry):
        energy_cols[o] = column(rows(o)[0]).astype(jnp.bfloat16)
        return carry

    lax.fori_loop(0, orbitals, spread, 0)

    def one_centre(slot, carry):
        o = centre[slot]
        sums[...] = jnp.zeros_like(sums)
        turned[...] = block(o).T
        v, minus, domain = rows(o)
        kept = jnp.minimum(slot, near)
        domain_cols[kept] = column(domain)

        def step(t, carry):
            others = [item_o[slot, t * UNROLL + u] for u in range(UNROLL)]
            weights = [item_w[slot, t * UNROLL + u] for u in range(UNROLL)]
            matches, scaled = [], []
            for n, w in zip(others, weights):
                _, minus_n, domain_n = rows(n)
                integ = mm(block(n), turned[...], NN)
                denom = wide(energy_cols[n]) + (v + minus + minus_n)
                amp = (integ * w) * pl.reciprocal(denom, approx=True)
                scaled.append(amp.astype(jnp.bfloat16))
                matches.append(hits(wide(domain_cols[kept]), domain_n))
            match = jnp.concatenate(matches, axis=1)
            sums[...] += mm(match, jnp.concatenate(scaled, axis=0), NN)
            return carry

        lax.fori_loop(0, (count[slot] + UNROLL - 1) // UNROLL, step, 0)
        mixes[slot] = sums[...].astype(jnp.bfloat16)
        return carry

    lax.fori_loop(0, used, one_centre, 0)
    for k in range(near):
        mixes[k] = mixes[k].T

    def one_pair(p):
        live = entry(0, me, p) >= 0
        i = jnp.where(live, entry(0, me, p), near_base)
        j = jnp.maximum(entry(1, me, p), 0)
        integ = mm(block(i), block(j), NT)
        v, minus, domain = rows(j)
        denom = wide(energy_cols[i]) + (v + minus + rows(i)[1])
        match = hits(wide(domain_cols[i - near_base]), domain)
        col_mix = mixes[jnp.maximum(slot_of[j], 0)]
        row_mix = mixes[i - near_base]
        both = jnp.concatenate([match, row_mix], axis=1)
        mixed = mm(both, jnp.concatenate([col_mix, match], axis=0), NN)
        amp = (mixed - integ) * pl.reciprocal(denom, approx=True)
        amp = jnp.where(live, amp, 0.0)
        amp_ref[p] = amp.astype(amp_ref.dtype)
        energy_ref[p] = jnp.sum(integ * amp) / (size * size)

    def second_step(t, carry):
        @pl.when(entry(0, me, t * PAIRS) >= 0)
        def _():
            for u in range(PAIRS):
                one_pair(t * PAIRS + u)

        @pl.when(entry(0, me, t * PAIRS) < 0)
        def _():
            for u in range(PAIRS):
                amp_ref[t * PAIRS + u] = jnp.zeros((size, size), amp_ref.dtype)
                energy_ref[t * PAIRS + u] = 0.0

        return carry

    lax.fori_loop(0, pair_dev // PAIRS, second_step, 0)


def gather_kernel(
    row_count,
    col_count,
    blocks_ref,
    virtual_ref,
    occupied_ref,
    domains_ref,
    pairs_ref,
    weight_ref,
    all_ref,
    meta_ref,
    own,
    own_meta,
    blocks_in,
    virtual_in,
    occupied_in,
    domains_in,
    pairs_in,
    weight_in,
    local_sem,
    load_sem,
    up_send,
    down_send,
    line_recv,
    side_send,
    side_recv,
    core_send,
    core_recv,
):
    row, col = lax.axis_index("row"), lax.axis_index("col")
    sources = (blocks_ref, virtual_ref, occupied_ref, domains_ref, pairs_ref, weight_ref)
    held = (blocks_in, virtual_in, occupied_in, domains_in, pairs_in, weight_in)
    loads = [
        pltpu.make_async_copy(src, dst, load_sem.at[k])
        for k, (src, dst) in enumerate(zip(sources, held))
    ]
    for c in loads:
        c.start()
    blocks_ref, virtual_ref, occupied_ref, domains_ref, pairs_ref, weight_ref = held
    occ_dev, fit, size = blocks_ref.shape
    levels = row_count // 2
    z, x = row // 2, row % 2

    def device(line, side, core):
        return {"row": line * 2 + side, "col": core}

    below, above = z > 0, z < levels - 1
    barrier = pltpu.get_barrier_semaphore()

    def greet(target):
        pl.semaphore_signal(barrier, inc=1, device_id=target, device_id_type=pl.DeviceIdType.MESH)

    greet(device(z, 1 - x, col))
    greet(device(z, x, 1 - col))

    @pl.when(below)
    def _():
        greet(device(z - 1, x, col))

    @pl.when(above)
    def _():
        greet(device(z + 1, x, col))

    for c in loads:
        c.wait()
    my_first = (row * col_count + col) * occ_dev
    r = lax.broadcasted_iota(jnp.int32, (FEAT, size), 0)
    for k in range(occ_dev):
        own[k, :size, :] = jnp.swapaxes(blocks_ref[k], 0, 1)
        v = virtual_ref[k : k + 1, :].astype(jnp.float32)
        o = occupied_ref[0:1, k : k + 1].astype(jnp.float32)
        dom = domains_ref[pl.ds(my_first + k, 1), :]
        high = (dom // 256).astype(jnp.float32)
        low = (dom % 256).astype(jnp.float32)
        rows = [v, 1.0, -o, 1.0, high, low, 1.0, 1.0]
        rows += [1.0, v, 1.0, -o, 256.0, 1.0, -256.0 * high, -low]
        out = jnp.zeros((FEAT, size), jnp.float32)
        for at, entry in enumerate(rows):
            out = jnp.where(r == at, entry, out)
        own[k, size:, :] = out.astype(own.dtype)
    slots = pairs_ref.shape[1]
    own_meta[...] = jnp.zeros_like(own_meta)
    own_meta[0:2, 0:slots] = pairs_ref[...].astype(jnp.float32)
    own_meta[2:3, 0:slots] = weight_ref[...]

    def index(line, side, core):
        return (line * 2 + side) * col_count + core

    me = index(z, x, col)
    keep = [
        pltpu.make_async_copy(own, all_ref.at[me], local_sem.at[0]),
        pltpu.make_async_copy(own_meta, meta_ref.at[me], local_sem.at[1]),
    ]
    for c in keep:
        c.start()
    neighbours = 2 + below.astype(jnp.int32) + above.astype(jnp.int32)
    pl.semaphore_wait(barrier, neighbours)

    def pair(slot, target, send, recv, at, mine=False):
        sources = (own, own_meta) if mine else (all_ref.at[slot], meta_ref.at[slot])
        return [
            pltpu.make_async_remote_copy(
                src_ref=sources[h],
                dst_ref=dst.at[slot],
                send_sem=send.at[at, h],
                recv_sem=recv.at[at, h],
                device_id=target,
                device_id_type=pl.DeviceIdType.MESH,
            )
            for h, dst in ((1, meta_ref), (0, all_ref))
        ]

    def start(copies):
        for c in copies:
            c.start()

    def sides(line, mine=False):
        start(pair(index(line, x, col), device(z, 1 - x, col), side_send, side_recv, line, mine))
        to_core(line, x, mine)

    def to_core(line, side, mine=False):
        at = line * 2 + side
        start(pair(index(line, side, col), device(z, x, 1 - col), core_send, core_recv, at, mine))

    def upward(line, mine=False):
        return pair(index(line, x, col), device(z + 1, x, col), up_send, line_recv, line, mine)

    def downward(line, mine=False):
        return pair(index(line, x, col), device(z - 1, x, col), down_send, line_recv, line, mine)

    def from_side(line):
        for c in pair(index(line, 1 - x, col), device(z, 1 - x, col), side_send, side_recv, line):
            c.wait_recv()
        to_core(line, 1 - x)

    @pl.when(above)
    def _():
        start(upward(z, True))

    @pl.when(below)
    def _():
        start(downward(z, True))

    sides(z, True)
    for s in range(1, levels):
        low, high = z - s, z + s

        @pl.when(low >= 0)
        def _():
            for c in upward(low):
                c.wait_recv()

            @pl.when(above)
            def _():
                start(upward(low))

            sides(low)

        @pl.when(high < levels)
        def _():
            for c in downward(high):
                c.wait_recv()

            @pl.when(below)
            def _():
                start(downward(high))

            sides(high)

        if s == 1:
            from_side(z)
        else:
            pl.when(z - (s - 1) >= 0)(lambda: from_side(z - (s - 1)))
            pl.when(z + (s - 1) < levels)(lambda: from_side(z + (s - 1)))
    last = levels - 1
    pl.when(z - last >= 0)(lambda: from_side(z - last))
    pl.when(z + last < levels)(lambda: from_side(z + last))
    for line in range(levels):
        for c in pair(index(line, x, col), device(z, 1 - x, col), side_send, side_recv, line):
            c.wait_send()
        for side in range(2):
            at = line * 2 + side
            slot = index(line, side, 1 - col)
            for c in pair(slot, device(z, x, 1 - col), core_send, core_recv, at):
                c.wait_recv()
                c.wait_send()

        @pl.when(above & (line <= z))
        def _():
            for c in upward(line):
                c.wait_send()

        @pl.when(below & (line >= z))
        def _():
            for c in downward(line):
                c.wait_send()

    for c in keep:
        c.wait()


def gather(blocks, virtual, occupied, domains, pair_list, coupling):
    row_count, col_count = lax.axis_size("row"), lax.axis_size("col")
    occ_dev, fit, size = blocks.shape
    devices = row_count * col_count
    levels = row_count // 2
    hbm = pl.BlockSpec(memory_space=pltpu.HBM)
    arguments = (blocks, virtual, occupied[None, :], domains, pair_list.T, coupling[None, :])
    unit, meta = (occ_dev, size + FEAT, fit), (8, 128)
    sems = pltpu.SemaphoreType.DMA
    return pl.pallas_call(
        functools.partial(gather_kernel, row_count, col_count),
        out_shape=(
            jax.ShapeDtypeStruct((devices,) + unit, jnp.bfloat16),
            jax.ShapeDtypeStruct((devices,) + meta, jnp.float32),
        ),
        in_specs=[hbm] * 6,
        out_specs=(hbm, hbm),
        scratch_shapes=[
            pltpu.VMEM(unit, jnp.bfloat16),
            pltpu.VMEM(meta, jnp.float32),
        ]
        + [pltpu.VMEM(a.shape, a.dtype) for a in arguments]
        + [sems((2,)), sems((6,))]
        + [sems((levels, 2))] * 5
        + [sems((row_count, 2))] * 2,
        compiler_params=pltpu.CompilerParams(
            collective_id=0, has_side_effects=True, vmem_limit_bytes=60 * 1024 * 1024
        ),
    )(*arguments)


def shards(blocks, virtual, occupied, domains, pair_list, coupling):
    row_count, col_count = lax.axis_size("row"), lax.axis_size("col")
    occ_dev, fit, size = blocks.shape
    pair_dev = pair_list.shape[0]
    gathered, meta = gather(blocks, virtual, occupied, domains, pair_list, coupling)
    all_blocks = gathered.reshape((-1,) + gathered.shape[2:])
    smem = pl.BlockSpec(memory_space=pltpu.SMEM)
    vmem = pl.BlockSpec(memory_space=pltpu.VMEM)
    near = col_count * occ_dev
    cap = max(near * row_count, col_count * pair_dev) + UNROLL
    return pl.pallas_call(
        functools.partial(pair_kernel, (row_count, col_count, occ_dev, pair_dev)),
        out_shape=(
            jax.ShapeDtypeStruct((pair_dev, size, size), jnp.bfloat16),
            jax.ShapeDtypeStruct((pair_dev,), jnp.float32),
        ),
        in_specs=[pl.BlockSpec(memory_space=pltpu.HBM)] * 2,
        out_specs=(vmem, smem),
        scratch_shapes=[
            pltpu.VMEM(all_blocks.shape, jnp.bfloat16),
            pltpu.VMEM((size, size), jnp.float32),
            pltpu.VMEM((near + pair_dev, size, size), jnp.bfloat16),
            pltpu.VMEM((fit, size), jnp.bfloat16),
            pltpu.VMEM((row_count * near, size, LANES), jnp.bfloat16),
            pltpu.VMEM((near + 1, size, LANES), jnp.float32),
            pltpu.SMEM((row_count * near,), jnp.int32),
            pltpu.SMEM((near + pair_dev + 1,), jnp.int32),
            pltpu.SMEM((near + pair_dev + 1,), jnp.int32),
            pltpu.SMEM((near + pair_dev + 1, cap), jnp.int32),
            pltpu.SMEM((near + pair_dev + 1, cap), jnp.float32),
            pltpu.SMEM(meta.shape, jnp.float32),
            pltpu.SemaphoreType.DMA,
            pltpu.SemaphoreType.DMA,
        ],
        compiler_params=pltpu.CompilerParams(vmem_limit_bytes=60 * 1024 * 1024),
    )(meta, all_blocks)


def solution(mesh):
    return jax.shard_map(
        shards,
        mesh=mesh,
        in_specs=(
            P(("grp", "row", "col"), None, None),
            P(("grp", "row", "col"), None),
            P(("grp", "row", "col")),
            P("grp", None),
            P(("grp", "row", "col"), None),
            P(("grp", "row", "col")),
        ),
        out_specs=(P(("grp", "row", "col"), None, None), P(("grp", "row", "col"))),
        check_vma=False,
    )
```

```python
import functools
import jax
import jax.numpy as jnp
from jax import lax
from jax.experimental import pallas as pl
from jax.experimental.pallas import tpu as pltpu
from jax.sharding import PartitionSpec as P

FEAT = 16
UNROLL = 4
PAIRS = 4
LANES = 128
NT = (((1,), (1,)), ((), ()))
NN = (((1,), (0,)), ((), ()))


def mm(a, b, dims):
    return lax.dot_general(a, b, dims, preferred_element_type=jnp.float32)


def pair_kernel(
    dims,
    meta_ref,
    gathered_ref,
    amp_ref,
    energy_ref,
    blocks_ref,
    sums,
    mixes,
    turned,
    energy_cols,
    domain_cols,
    slot_of,
    centre,
    count,
    item_o,
    item_w,
    meta,
    load_sem,
    meta_sem,
):
    row_count, col_count, occ_dev, pair_dev = dims
    my_row, my_col = lax.axis_index("row"), lax.axis_index("col")
    orbitals = row_count * col_count * occ_dev
    near = col_count * occ_dev
    size = amp_ref.shape[1]
    cap = item_o.shape[1]
    near_base = my_row * near
    load = pltpu.make_async_copy(gathered_ref, blocks_ref, load_sem)
    load.start()
    fetch = pltpu.make_async_copy(meta_ref, meta, meta_sem)
    fetch.start()
    trash = near + pair_dev

    def clear(j, carry):
        slot_of[j] = -1
        return carry

    lax.fori_loop(0, orbitals, clear, 0)
    for k in range(near):
        centre[k] = near_base + k
    for k in range(near + pair_dev + 1):
        count[k] = 0
    fetch.wait()
    me = my_row * col_count + my_col

    def entry(row, device, q):
        return meta[device, row, q].astype(jnp.int32)

    used = jnp.int32(near)
    for p in range(pair_dev):
        live = entry(0, me, p) >= 0
        j = jnp.maximum(entry(1, me, p), 0)
        known = slot_of[j]
        fresh = live & (known < 0)
        slot_of[j] = jnp.where(fresh, used, known)
        centre[jnp.where(fresh, used, trash)] = j
        used = used + fresh.astype(jnp.int32)

    def add(take, slot, orbital, w):
        slot = jnp.where(take, slot, trash)
        n = count[slot]
        item_o[slot, n] = orbital
        item_w[slot, n] = -w
        count[slot] = n + take.astype(jnp.int32)

    def col_items(owner, carry):
        device = owner * col_count + my_col
        for q in range(pair_dev):
            i = entry(0, device, q)
            slot = slot_of[jnp.maximum(entry(1, device, q), 0)]
            add((i >= 0) & (slot >= 0), slot, i, meta[device, 2, q])
        return carry

    lax.fori_loop(0, row_count, col_items, 0)

    def row_items(side, carry):
        device = my_row * col_count + side
        for q in range(pair_dev):
            i = entry(0, device, q)
            add(i >= 0, i - near_base, entry(1, device, q), meta[device, 2, q])
        return carry

    lax.fori_loop(0, col_count, row_items, 0)

    def pad(slot, carry):
        n = count[slot]
        for u in range(UNROLL):
            item_o[slot, n + u] = 0
            item_w[slot, n + u] = 0.0
        return carry

    lax.fori_loop(0, used, pad, 0)
    load.wait()

    def block(o):
        return blocks_ref[o, :size, :]

    def rows(o):
        f = blocks_ref[o, size:, :].astype(jnp.float32)
        return f[9:10], f[11:12], -(f[14:15] + f[15:16])

    def column(row):
        return jnp.broadcast_to(row, (LANES, size)).T

    def wide(col):
        return jnp.concatenate([col.astype(jnp.float32)] * (size // LANES), axis=1)

    def hits(col, row):
        return jnp.where(col == row, 1.0, 0.0).astype(jnp.bfloat16)

    def spread(t, carry):
        for u in range(2 * near):
            o = t * 2 * near + u
            energy_cols[o] = column(rows(o)[0]).astype(jnp.bfloat16)
        return carry

    lax.fori_loop(0, row_count // 2, spread, 0)

    def one_centre(slot, carry):
        o = centre[slot]
        sums[...] = jnp.zeros_like(sums)
        turned[...] = block(o).T
        v, minus, domain = rows(o)
        kept = jnp.minimum(slot, near)
        domain_cols[kept] = column(domain)

        def step(t, carry):
            others = [item_o[slot, t * UNROLL + u] for u in range(UNROLL)]
            weights = [item_w[slot, t * UNROLL + u] for u in range(UNROLL)]
            matches, scaled = [], []
            for n, w in zip(others, weights):
                _, minus_n, domain_n = rows(n)
                integ = mm(block(n), turned[...], NN)
                denom = wide(energy_cols[n]) + (v + minus + minus_n)
                amp = (integ * w) * pl.reciprocal(denom, approx=True)
                scaled.append(amp.astype(jnp.bfloat16))
                matches.append(hits(wide(domain_cols[kept]), domain_n))
            match = jnp.concatenate(matches, axis=1)
            sums[...] += mm(match, jnp.concatenate(scaled, axis=0), NN)
            return carry

        lax.fori_loop(0, (count[slot] + UNROLL - 1) // UNROLL, step, 0)
        mixes[slot] = sums[...].astype(jnp.bfloat16)
        return carry

    lax.fori_loop(0, used, one_centre, 0)
    for k in range(near):
        mixes[k] = mixes[k].T

    def one_pair(p):
        live = entry(0, me, p) >= 0
        i = jnp.where(live, entry(0, me, p), near_base)
        j = jnp.maximum(entry(1, me, p), 0)
        integ = mm(block(i), block(j), NT)
        v, minus, domain = rows(j)
        denom = wide(energy_cols[i]) + (v + minus + rows(i)[1])
        match = hits(wide(domain_cols[i - near_base]), domain)
        col_mix = mixes[jnp.maximum(slot_of[j], 0)]
        row_mix = mixes[i - near_base]
        both = jnp.concatenate([match, row_mix], axis=1)
        mixed = mm(both, jnp.concatenate([col_mix, match], axis=0), NN)
        amp = (mixed - integ) * pl.reciprocal(denom, approx=True)
        amp = jnp.where(live, amp, 0.0)
        amp_ref[p] = amp.astype(amp_ref.dtype)
        energy_ref[p] = jnp.sum(integ * amp) / (size * size)

    def second_step(t, carry):
        @pl.when(entry(0, me, t * PAIRS) >= 0)
        def _():
            for u in range(PAIRS):
                one_pair(t * PAIRS + u)

        @pl.when(entry(0, me, t * PAIRS) < 0)
        def _():
            for u in range(PAIRS):
                amp_ref[t * PAIRS + u] = jnp.zeros((size, size), amp_ref.dtype)
                energy_ref[t * PAIRS + u] = 0.0

        return carry

    lax.fori_loop(0, pair_dev // PAIRS, second_step, 0)


def gather_kernel(
    row_count,
    col_count,
    blocks_ref,
    virtual_ref,
    occupied_ref,
    domains_ref,
    pairs_ref,
    weight_ref,
    all_ref,
    meta_ref,
    own,
    own_meta,
    blocks_in,
    virtual_in,
    occupied_in,
    domains_in,
    pairs_in,
    weight_in,
    local_sem,
    load_sem,
    up_send,
    down_send,
    line_recv,
    side_send,
    side_recv,
    core_send,
    core_recv,
):
    row, col = lax.axis_index("row"), lax.axis_index("col")
    sources = (blocks_ref, virtual_ref, occupied_ref, domains_ref, pairs_ref, weight_ref)
    held = (blocks_in, virtual_in, occupied_in, domains_in, pairs_in, weight_in)
    loads = [
        pltpu.make_async_copy(src, dst, load_sem.at[k])
        for k, (src, dst) in enumerate(zip(sources, held))
    ]
    for c in loads:
        c.start()
    blocks_ref, virtual_ref, occupied_ref, domains_ref, pairs_ref, weight_ref = held
    occ_dev, fit, size = blocks_ref.shape
    levels = row_count // 2
    z, x = row // 2, row % 2

    def device(line, side, core):
        return {"row": line * 2 + side, "col": core}

    below, above = z > 0, z < levels - 1
    barrier = pltpu.get_barrier_semaphore()

    def greet(target):
        pl.semaphore_signal(barrier, inc=1, device_id=target, device_id_type=pl.DeviceIdType.MESH)

    greet(device(z, 1 - x, col))
    greet(device(z, x, 1 - col))

    @pl.when(below)
    def _():
        greet(device(z - 1, x, col))

    @pl.when(above)
    def _():
        greet(device(z + 1, x, col))

    for c in loads:
        c.wait()
    my_first = (row * col_count + col) * occ_dev
    r = lax.broadcasted_iota(jnp.int32, (FEAT, size), 0)
    for k in range(occ_dev):
        own[k, :size, :] = jnp.swapaxes(blocks_ref[k], 0, 1)
        v = virtual_ref[k : k + 1, :].astype(jnp.float32)
        o = occupied_ref[0:1, k : k + 1].astype(jnp.float32)
        dom = domains_ref[pl.ds(my_first + k, 1), :]
        high = (dom // 256).astype(jnp.float32)
        low = (dom % 256).astype(jnp.float32)
        rows = [v, 1.0, -o, 1.0, high, low, 1.0, 1.0]
        rows += [1.0, v, 1.0, -o, 256.0, 1.0, -256.0 * high, -low]
        out = jnp.zeros((FEAT, size), jnp.float32)
        for at, entry in enumerate(rows):
            out = jnp.where(r == at, entry, out)
        own[k, size:, :] = out.astype(own.dtype)
    slots = pairs_ref.shape[1]
    own_meta[...] = jnp.zeros_like(own_meta)
    own_meta[0:2, 0:slots] = pairs_ref[...].astype(jnp.float32)
    own_meta[2:3, 0:slots] = weight_ref[...]

    def index(line, side, core):
        return (line * 2 + side) * col_count + core

    me = index(z, x, col)
    keep = [
        pltpu.make_async_copy(own, all_ref.at[me], local_sem.at[0]),
        pltpu.make_async_copy(own_meta, meta_ref.at[me], local_sem.at[1]),
    ]
    for c in keep:
        c.start()
    neighbours = 2 + below.astype(jnp.int32) + above.astype(jnp.int32)
    pl.semaphore_wait(barrier, neighbours)

    def pair(slot, target, send, recv, at, mine=False):
        sources = (own, own_meta) if mine else (all_ref.at[slot], meta_ref.at[slot])
        return [
            pltpu.make_async_remote_copy(
                src_ref=sources[h],
                dst_ref=dst.at[slot],
                send_sem=send.at[at, h],
                recv_sem=recv.at[at, h],
                device_id=target,
                device_id_type=pl.DeviceIdType.MESH,
            )
            for h, dst in ((1, meta_ref), (0, all_ref))
        ]

    def start(copies):
        for c in copies:
            c.start()

    def sides(line, mine=False):
        start(pair(index(line, x, col), device(z, 1 - x, col), side_send, side_recv, line, mine))
        to_core(line, x, mine)

    def to_core(line, side, mine=False):
        at = line * 2 + side
        start(pair(index(line, side, col), device(z, x, 1 - col), core_send, core_recv, at, mine))

    def upward(line, mine=False):
        return pair(index(line, x, col), device(z + 1, x, col), up_send, line_recv, line, mine)

    def downward(line, mine=False):
        return pair(index(line, x, col), device(z - 1, x, col), down_send, line_recv, line, mine)

    def from_side(line):
        for c in pair(index(line, 1 - x, col), device(z, 1 - x, col), side_send, side_recv, line):
            c.wait_recv()
        to_core(line, 1 - x)

    @pl.when(above)
    def _():
        start(upward(z, True))

    @pl.when(below)
    def _():
        start(downward(z, True))

    sides(z, True)
    for s in range(1, levels):
        low, high = z - s, z + s

        @pl.when(low >= 0)
        def _():
            for c in upward(low):
                c.wait_recv()

            @pl.when(above)
            def _():
                start(upward(low))

            sides(low)

        @pl.when(high < levels)
        def _():
            for c in downward(high):
                c.wait_recv()

            @pl.when(below)
            def _():
                start(downward(high))

            sides(high)

        if s == 1:
            from_side(z)
        else:
            pl.when(z - (s - 1) >= 0)(lambda: from_side(z - (s - 1)))
            pl.when(z + (s - 1) < levels)(lambda: from_side(z + (s - 1)))
    last = levels - 1
    pl.when(z - last >= 0)(lambda: from_side(z - last))
    pl.when(z + last < levels)(lambda: from_side(z + last))
    for line in range(levels):
        for c in pair(index(line, x, col), device(z, 1 - x, col), side_send, side_recv, line):
            c.wait_send()
        for side in range(2):
            at = line * 2 + side
            slot = index(line, side, 1 - col)
            for c in pair(slot, device(z, x, 1 - col), core_send, core_recv, at):
                c.wait_recv()
                c.wait_send()

        @pl.when(above & (line <= z))
        def _():
            for c in upward(line):
                c.wait_send()

        @pl.when(below & (line >= z))
        def _():
            for c in downward(line):
                c.wait_send()

    for c in keep:
        c.wait()


def gather(blocks, virtual, occupied, domains, pair_list, coupling):
    row_count, col_count = lax.axis_size("row"), lax.axis_size("col")
    occ_dev, fit, size = blocks.shape
    devices = row_count * col_count
    levels = row_count // 2
    hbm = pl.BlockSpec(memory_space=pltpu.HBM)
    arguments = (blocks, virtual, occupied[None, :], domains, pair_list.T, coupling[None, :])
    unit, meta = (occ_dev, size + FEAT, fit), (8, 128)
    sems = pltpu.SemaphoreType.DMA
    return pl.pallas_call(
        functools.partial(gather_kernel, row_count, col_count),
        out_shape=(
            jax.ShapeDtypeStruct((devices,) + unit, jnp.bfloat16),
            jax.ShapeDtypeStruct((devices,) + meta, jnp.float32),
        ),
        in_specs=[hbm] * 6,
        out_specs=(hbm, hbm),
        scratch_shapes=[
            pltpu.VMEM(unit, jnp.bfloat16),
            pltpu.VMEM(meta, jnp.float32),
        ]
        + [pltpu.VMEM(a.shape, a.dtype) for a in arguments]
        + [sems((2,)), sems((6,))]
        + [sems((levels, 2))] * 5
        + [sems((row_count, 2))] * 2,
        compiler_params=pltpu.CompilerParams(
            collective_id=0, has_side_effects=True, vmem_limit_bytes=60 * 1024 * 1024
        ),
    )(*arguments)


def shards(blocks, virtual, occupied, domains, pair_list, coupling):
    row_count, col_count = lax.axis_size("row"), lax.axis_size("col")
    occ_dev, fit, size = blocks.shape
    pair_dev = pair_list.shape[0]
    gathered, meta = gather(blocks, virtual, occupied, domains, pair_list, coupling)
    all_blocks = gathered.reshape((-1,) + gathered.shape[2:])
    smem = pl.BlockSpec(memory_space=pltpu.SMEM)
    vmem = pl.BlockSpec(memory_space=pltpu.VMEM)
    near = col_count * occ_dev
    cap = max(near * row_count, col_count * pair_dev) + UNROLL
    return pl.pallas_call(
        functools.partial(pair_kernel, (row_count, col_count, occ_dev, pair_dev)),
        out_shape=(
            jax.ShapeDtypeStruct((pair_dev, size, size), jnp.bfloat16),
            jax.ShapeDtypeStruct((pair_dev,), jnp.float32),
        ),
        in_specs=[pl.BlockSpec(memory_space=pltpu.HBM)] * 2,
        out_specs=(vmem, smem),
        scratch_shapes=[
            pltpu.VMEM(all_blocks.shape, jnp.bfloat16),
            pltpu.VMEM((size, size), jnp.float32),
            pltpu.VMEM((near + pair_dev, size, size), jnp.bfloat16),
            pltpu.VMEM((fit, size), jnp.bfloat16),
            pltpu.VMEM((row_count * near, size, LANES), jnp.bfloat16),
            pltpu.VMEM((near + 1, size, LANES), jnp.float32),
            pltpu.SMEM((row_count * near,), jnp.int32),
            pltpu.SMEM((near + pair_dev + 1,), jnp.int32),
            pltpu.SMEM((near + pair_dev + 1,), jnp.int32),
            pltpu.SMEM((near + pair_dev + 1, cap), jnp.int32),
            pltpu.SMEM((near + pair_dev + 1, cap), jnp.float32),
            pltpu.SMEM(meta.shape, jnp.float32),
            pltpu.SemaphoreType.DMA,
            pltpu.SemaphoreType.DMA,
        ],
        compiler_params=pltpu.CompilerParams(vmem_limit_bytes=60 * 1024 * 1024),
    )(meta, all_blocks)


def solution(mesh):
    return jax.shard_map(
        shards,
        mesh=mesh,
        in_specs=(
            P(("grp", "row", "col"), None, None),
            P(("grp", "row", "col"), None),
            P(("grp", "row", "col")),
            P("grp", None),
            P(("grp", "row", "col"), None),
            P(("grp", "row", "col")),
        ),
        out_specs=(P(("grp", "row", "col"), None, None), P(("grp", "row", "col"))),
        check_vma=False,
    )
```
